128 devices in a mesh: pop: 8 (over z, y_lo), mp: 16 (over x, y_hi, core).
Axes of the slice: x: 4, y: 4 (y_hi: 2, y_lo: 2; y = y_hi * 2 + y_lo), z: 4, core: 2. Of those that a mesh axis runs over, the one named last changes fastest.
Arguments:
- tokens: bfloat16 [4096, 3584], P('pop', 'mp'), may hold values from -6 to 6
- w_gate: bfloat16 [3584, 18944], P(None, 'mp'), may hold values from -0.09375 to 0.09375
- w_up: bfloat16 [3584, 18944], P(None, 'mp'), may hold values from -0.09375 to 0.09375
- a_gate: bfloat16 [2048, 4, 3584], P('pop', None, 'mp'), may hold values from -0.125 to 0.125
- a_up: bfloat16 [2048, 4, 3584], P('pop', None, 'mp'), may hold values from -0.09375 to 0.09375
- b_gate: bfloat16 [2048, 4, 18944], P('pop', None, 'mp'), may hold values from -6 to 6
- b_up: bfloat16 [2048, 4, 18944], P('pop', None, 'mp'), may hold values from -6 to 6
- fitness: float32 [2048], P('pop'), may hold values from -4 to 4
Outputs:
- hidden: bfloat16 [4096, 18944], P('pop', 'mp')
- new_gate: bfloat16 [3584, 18944], P('pop', 'mp')
- new_up: bfloat16 [3584, 18944], P('pop', 'mp')
The draws below stay inside these ranges and needn't reach their ends.
All inputs are finite; a program needn't handle non-finite values.
Results may differ from the reference program's by a relative error of at most 0.015.
Values may be sent and summed in bfloat16 or wider, within the bound.
No kernel may reach another device: no remote copies, remote signals or barrier semaphores. Data moves between devices by JAX's collectives and lax.ppermute only.
A program may use at most 192 MiB of HBM per device.

```python
import jax
import jax.numpy as jnp
from jax import lax

D = 3584
FEEDFORWARD_DIM = 18944
RANK = 4
MEMBERS = 2048
TOKENS = 4096
N_POP = 8


def raised(values, own_key, source, target, blocks, factor):
    def block_of(axis_at):
        return (jnp.arange(values.shape[axis_at]) // (values.shape[axis_at] // blocks)).reshape((-1,) + (1,) * (values.ndim - 1 - axis_at))

    near = jax.random.permutation(own_key, blocks)[block_of(target)]
    other_side = (block_of(target) + blocks // 2) % blocks
    return jnp.where((block_of(source) == near) | (block_of(source) == other_side), factor * values, values)


def level_of(stream_key, dims, cuts, low, top_value):
    level = 1.0
    for axis_at, parts in cuts:
        steps = jax.random.uniform(jax.random.fold_in(jax.random.fold_in(stream_key, 6), axis_at), (parts,), jnp.float32, low / len(cuts), top_value / len(cuts))
        level = level * jnp.repeat(jnp.exp(steps), dims[axis_at] // parts).reshape((-1,) + (1,) * (len(dims) - 1 - axis_at))
    return level


def scatter_about(key, shape, scale, bound, pieces=(), kind=jnp.bfloat16):
    factor_of = level_of(key, shape, pieces, -0.22, 0.18) if pieces else 1.0
    array = jax.random.normal(key, shape, jnp.float32) * scale * factor_of
    return jnp.minimum(jnp.maximum(array, -bound), bound).astype(kind)


def heavy_noise(own_key, extent, width, most, shards, heavy, held_as=jnp.bfloat16):
    values = width * jax.random.normal(own_key, extent, jnp.float32)
    if shards:
        values = values * level_of(own_key, extent, shards, -0.22, 0.18)
    return jnp.clip(raised(values, jax.random.fold_in(own_key, 3), *heavy), -most, most).astype(held_as)


def setup_inputs(seed: int = 0) -> dict:
    splits = jax.random.split(jax.random.key(seed), 9)
    return {
        "tokens": scatter_about(splits[0], (TOKENS, D), 1.0, 6.0, ((0, 8), (1, 16))),
        "w_gate": scatter_about(splits[1], (D, FEEDFORWARD_DIM), D ** -0.5, 0.09375, ((1, 16),)),
        "w_up": scatter_about(splits[2], (D, FEEDFORWARD_DIM), D ** -0.5, 0.09375, ((1, 16),)),
        "a_gate": heavy_noise(splits[3], (MEMBERS, RANK, D), D ** -0.5, 0.125, ((0, 8), (2, 16)), (0, 2, 16, 2.0)),
        "a_up": scatter_about(splits[4], (MEMBERS, RANK, D), D ** -0.5, 0.09375, ((0, 8), (2, 16))),
        "b_gate": scatter_about(splits[5], (MEMBERS, RANK, FEEDFORWARD_DIM), 1.0, 6.0, ((0, 8), (2, 16))),
        "b_up": scatter_about(splits[6], (MEMBERS, RANK, FEEDFORWARD_DIM), 1.0, 6.0, ((0, 8), (2, 16))),
        "fitness": scatter_about(splits[7], (MEMBERS,), 1.0, 4.0, ((0, 8),), jnp.float32),
    }


noise_scale = 0.5

def project_pair(tokens, weight, a_fac, second_factor, member_list):
    paired = tokens.reshape(member_list, 2, D).astype(jnp.float32)
    probe_vector = jnp.einsum('mtd,mrd->mtr', paired, a_fac.astype(jnp.float32)).astype(jnp.bfloat16)
    lowrank_noise = jnp.einsum('axg,agq->axq', probe_vector.astype(jnp.float32), second_factor.astype(jnp.float32)).reshape(2 * member_list, FEEDFORWARD_DIM)
    base_part = jnp.dot(tokens, weight, preferred_element_type=jnp.float32)
    return base_part + noise_scale * lowrank_noise

def update_one(weight, a_fac, second_factor, fitness, member_list):
    scaled = (fitness[:, None, None] * a_fac.astype(jnp.float32)).astype(jnp.bfloat16)
    step_coeff = 1.0 / jnp.sqrt(jnp.float32(member_list * RANK))
    group_size = member_list // N_POP
    total = jnp.zeros((D, FEEDFORWARD_DIM), jnp.float32)
    for group in range(N_POP):
        left_side = scaled[group * group_size:(group + 1) * group_size].reshape(group_size * RANK, D).astype(jnp.float32)
        right_side = second_factor[group * group_size:(group + 1) * group_size].reshape(group_size * RANK, FEEDFORWARD_DIM).astype(jnp.float32)
        running_sum = step_coeff * jnp.dot(left_side.T, right_side, precision=lax.Precision.HIGHEST)
        rounded = lax.optimization_barrier(running_sum.astype(jnp.bfloat16))
        total = total + rounded.astype(jnp.float32)
    return (weight.astype(jnp.float32) + total).astype(jnp.bfloat16)

def reference(tokens, w_gate, w_up, a_gate, a_up, b_gate, b_up, fitness):
    member_list = a_gate.shape[0]
    gate_pre = project_pair(tokens, w_gate, a_gate, b_gate, member_list)
    up_pre = project_pair(tokens, w_up, a_up, b_up, member_list)
    hidden = (jax.nn.silu(gate_pre) * up_pre).astype(jnp.bfloat16)
    new_gate = update_one(w_gate, a_gate, b_gate, fitness, member_list)
    new_up = update_one(w_up, a_up, b_up, fitness, member_list)
    return (hidden, new_gate, new_up)
```

```python
import functools

import jax
import jax.numpy as jnp
from jax import lax
from jax.experimental import pallas as pl
from jax.experimental.pallas import tpu as pltpu
from jax.sharding import Mesh
from jax.sharding import PartitionSpec as P

bf16 = jnp.bfloat16
f32 = jnp.float32
noise_scale = 0.5
AXES = ("z", "l", "x", "h", "c")
VMEM = 56 * 1024 * 1024


def _params():
    return pltpu.CompilerParams(vmem_limit_bytes=VMEM)


def _own_mask(members, tokens):
    m = lax.broadcasted_iota(jnp.int32, (members, tokens), 0)
    t = lax.broadcasted_iota(jnp.int32, (members, tokens), 1)
    return jnp.logical_or(t == 2 * m, t == 2 * m + 1)


def _probe_kernel(tok_ref, ag_ref, au_ref, out_ref):
    tok = tok_ref[...]
    mask = _own_mask(ag_ref.shape[2], tok.shape[1])
    rows = []
    for ref in (ag_ref, au_ref):
        for r in range(ref.shape[0]):
            s = lax.dot_general(ref[r], tok, (((0,), (0,)), ((), ())), preferred_element_type=f32)
            rows.append(jnp.sum(jnp.where(mask, s, 0.0), axis=0, keepdims=True))
    out_ref[...] = jnp.concatenate(rows, axis=0)


def probes(tok_t, ag, au):
    return pl.pallas_call(
        _probe_kernel,
        out_shape=jax.ShapeDtypeStruct((2 * ag.shape[0], tok_t.shape[1]), f32),
        compiler_params=_params(),
        name="probes",
    )(tok_t, ag, au)


def _update_kernel(coeff, own_ref, oth_ref, b0_ref, b1_ref, out_ref):
    rank = b0_ref.shape[0]
    rhs = jnp.concatenate([b0_ref[r] for r in range(rank)] + [b1_ref[r] for r in range(rank)], axis=1)
    rows = []
    for ref in (own_ref, oth_ref):
        rows.append(jnp.concatenate([ref[0, s, r] for s in range(2) for r in range(rank)], axis=1))
    lhs = jnp.concatenate(rows, axis=0)
    acc = lax.dot_general(lhs, rhs, (((1,), (1,)), ((), ())), preferred_element_type=f32)
    out_ref[0] = (acc * coeff).astype(out_ref.dtype)


def update(coeff, own, oth, b0, b1):
    nx, _, rank, d, m = own.shape
    q = b0.shape[1]
    a_spec = pl.BlockSpec((1, 2, rank, d, m), lambda i: (i, 0, 0, 0, 0))
    b_spec = pl.BlockSpec((rank, q, m), lambda i: (0, 0, 0))
    return pl.pallas_call(
        functools.partial(_update_kernel, coeff),
        grid=(nx,),
        in_specs=[a_spec, a_spec, b_spec, b_spec],
        out_specs=pl.BlockSpec((1, 2 * d, q), lambda i: (i, 0, 0)),
        out_shape=jax.ShapeDtypeStruct((nx, 2 * d, q), bf16),
        compiler_params=_params(),
        cost_estimate=pl.CostEstimate(
            flops=2 * nx * 2 * d * 2 * rank * m * q,
            bytes_accessed=2 * (4 * nx * rank * d * m + 2 * rank * q * m + nx * 2 * d * q),
            transcendentals=0,
        ),
        name="update",
    )(own, oth, b0, b1)


def _hidden_kernel(tok_ref, probe_ref, wg_ref, wu_ref, bg_ref, bu_ref, out_ref, p_ref):
    rank, _, m = bg_ref.shape
    t = tok_ref.shape[1]

    @pl.when(pl.program_id(0) == 0)
    def _():
        mask = _own_mask(m, t)
        for i in range(2 * rank):
            row = (probe_ref[i : i + 1, :].astype(bf16).astype(f32)) * noise_scale
            p_ref[i * m : (i + 1) * m, :] = jnp.where(mask, jnp.broadcast_to(row, (m, t)), 0.0).astype(bf16)

    tok = tok_ref[...]
    pre = []
    for k, (w_ref, b_ref) in enumerate(((wg_ref, bg_ref), (wu_ref, bu_ref))):
        b = jnp.concatenate([b_ref[r] for r in range(rank)], axis=1)
        acc = jnp.dot(w_ref[...], tok, preferred_element_type=f32)
        acc += jnp.dot(b, p_ref[k * rank * m : (k + 1) * rank * m, :], preferred_element_type=f32)
        pre.append(acc)
    g, u = pre
    out_ref[...] = (g / (1.0 + jnp.exp(-g)) * u).astype(out_ref.dtype)


def hidden_of(tok, probe, wg, wu, bg, bu):
    d, t = tok.shape
    q = wg.shape[0]
    rank, _, m = bg.shape
    block = 304
    w_spec = pl.BlockSpec((block, d), lambda i: (i, 0))
    b_spec = pl.BlockSpec((rank, block, m), lambda i: (0, i, 0))
    return pl.pallas_call(
        _hidden_kernel,
        grid=(pl.cdiv(q, block),),
        in_specs=[
            pl.BlockSpec((d, t), lambda i: (0, 0)),
            pl.BlockSpec((2 * rank, t), lambda i: (0, 0)),
            w_spec,
            w_spec,
            b_spec,
            b_spec,
        ],
        out_specs=pl.BlockSpec((block, t), lambda i: (i, 0)),
        out_shape=jax.ShapeDtypeStruct((q, t), bf16),
        scratch_shapes=[pltpu.VMEM((2 * rank * m, t), bf16)],
        compiler_params=_params(),
        cost_estimate=pl.CostEstimate(
            flops=4 * q * t * (d + rank * m),
            bytes_accessed=2 * (2 * q * d + d * t + 2 * rank * q * m + q * t),
            transcendentals=q * t,
        ),
        name="hidden",
    )(tok, probe, wg, wu, bg, bu)


def swap(v, axis, shift=1):
    n = lax.axis_size(axis)
    return lax.ppermute(v, axis, [(i, (i + shift) % n) for i in range(n)])


def local(tokens, w_gate, w_up, a_gate, a_up, b_gate, b_up, fitness):
    members, rank, d_own = a_gate.shape
    q = w_gate.shape[1]
    pops = lax.axis_size("z") * lax.axis_size("l")
    coeff = 1.0 / (members * pops * rank) ** 0.5
    h, l, c = lax.axis_index("h"), lax.axis_index("l"), lax.axis_index("c")
    y = 2 * h + l
    at_y = (0, 2, 1, 3)
    tok_t = tokens.T
    a_t = [a.transpose(1, 2, 0) for a in (a_gate, a_up)]
    b_t = [b.transpose(1, 2, 0) for b in (b_gate, b_up)]
    cuts = ((0, 640), (640, q))

    def factors(a):
        s = (a.astype(f32) * fitness[None, None, :]).astype(bf16)
        pa = lax.ppermute(s, ("l", "h"), [(at_y[i], at_y[j]) for i, j in ((1, 0), (2, 1), (0, 2))])
        pb = lax.ppermute(s, ("l", "h"), [(at_y[i], at_y[j]) for i, j in ((3, 1), (1, 2), (2, 3))])
        mine = jnp.where(y == 1, pb, jnp.where(y == 2, pa, s))
        other = jnp.where(y < 2, pa, pb)
        both = jnp.stack([mine, other])
        own = lax.all_gather(both, "x", axis=0, tiled=False)
        return own, swap(own, "c")

    part = probes(tok_t, *a_t)
    part = part + swap(part, "c")
    part = part + swap(part, "h")
    part = part + lax.ppermute(part, "x", [(i, i ^ 1) for i in range(4)])
    part = part + lax.ppermute(part, "x", [(i, i ^ 2) for i in range(4)])

    sums = []
    for a, b in zip(a_t, b_t):
        own, oth = factors(a)
        pieces = []
        for lo, hi in cuts:
            b0 = lax.slice_in_dim(b, lo, hi, axis=1)
            b1 = swap(b0, "l")
            prod = update(coeff, own, oth, b0, b1)
            prod = prod.reshape(prod.shape[0] * prod.shape[1], hi - lo)
            pieces.append(lax.psum_scatter(prod, "z", scatter_dimension=0, tiled=True))
        sums.append(pieces)

    near = jnp.stack([tok_t, swap(tok_t, "h")])
    near = jnp.where(h == 0, near, near[::-1])
    mine = lax.all_gather(near, "x", axis=0, tiled=False)
    other = swap(mine, "c")
    tok = jnp.where(c == 0, jnp.stack([mine, other], axis=2), jnp.stack([other, mine], axis=2))
    tok = tok.reshape(-1, tok_t.shape[1])
    hidden = hidden_of(tok, part, w_gate.T, w_up.T, *b_t).T

    rows = 2 * d_own
    first = (lax.axis_index("z") * 2 + l) * rows
    news = []
    for w, pieces in zip((w_gate, w_up), sums):
        keep = lax.dynamic_slice_in_dim(w, first, rows, 0).astype(f32)
        total = jnp.concatenate(pieces, axis=1)
        total = jnp.where(c == 0, total, jnp.concatenate([total[d_own:], total[:d_own]], axis=0))
        news.append((keep + total.astype(f32)).astype(bf16))
    return hidden, news[0], news[1]


def solution(mesh):
    fine = Mesh(mesh.devices.reshape(4, 2, 4, 2, 2), AXES)
    pop, mp = ("z", "l"), ("x", "h", "c")
    return jax.shard_map(
        local,
        mesh=fine,
        in_specs=(
            P(pop, mp),
            P(None, mp),
            P(None, mp),
            P(pop, None, mp),
            P(pop, None, mp),
            P(pop, None, mp),
            P(pop, None, mp),
            P(pop),
        ),
        out_specs=(P(pop, mp), P(pop, mp), P(pop, mp)),
        check_vma=False,
    )
```

```python
import functools

import jax
import jax.numpy as jnp
from jax import lax
from jax.experimental import pallas as pl
from jax.experimental.pallas import tpu as pltpu
from jax.sharding import Mesh
from jax.sharding import PartitionSpec as P

bf16 = jnp.bfloat16
f32 = jnp.float32
noise_scale = 0.5
AXES = ("z", "l", "x", "h", "c")
RING = 4
VMEM = 58 * 1024 * 1024
NT = (((1,), (1,)), ((), ()))
TN = (((0,), (0,)), ((), ()))


def _call(kernel, name, flops=0, moved=0, **kw):
    return pl.pallas_call(
        kernel,
        name=name,
        compiler_params=pltpu.CompilerParams(vmem_limit_bytes=VMEM),
        cost_estimate=pl.CostEstimate(flops=flops, bytes_accessed=moved, transcendentals=0),
        **kw,
    )


def _any(n):
    return [pl.BlockSpec(memory_space=pl.ANY)] * n


FULL = pl.BlockSpec(memory_space=pltpu.VMEM)
SCALARS = pl.BlockSpec(memory_space=pltpu.SMEM)


def swap(v, axis, shift=1):
    n = lax.axis_size(axis)
    return lax.ppermute(v, axis, [(i, (i + shift) % n) for i in range(n)])


def tie(v, *after):
    return _call(
        lambda *refs: None,
        "tie",
        in_specs=_any(1 + len(after)),
        out_specs=pl.BlockSpec(memory_space=pl.ANY),
        out_shape=jax.ShapeDtypeStruct(v.shape, v.dtype),
        input_output_aliases={0: 0},
    )(v, *after)


def _own_mask(members, tokens):
    m = lax.broadcasted_iota(jnp.int32, (members, tokens), 0)
    t = lax.broadcasted_iota(jnp.int32, (members, tokens), 1)
    return jnp.logical_or(t == 2 * m, t == 2 * m + 1)


def _pack_kernel(tok_ref, ag_ref, au_ref, fit_ref, sg_ref, su_ref, pay_ref):
    rank, d, m = ag_ref.shape
    tok = tok_ref[...]
    t = tok.shape[1]
    fit = fit_ref[...]
    mask = _own_mask(m, t)
    rows = []
    for a_ref, s_ref in ((ag_ref, sg_ref), (au_ref, su_ref)):
        for r in range(rank):
            a = a_ref[r]
            s_ref[r * d : (r + 1) * d, :] = (a.astype(f32) * fit).astype(bf16)
            s = lax.dot_general(a, tok, TN, preferred_element_type=f32)
            rows.append(jnp.sum(jnp.where(mask, s, 0.0), axis=0, keepdims=True))
    part = jnp.concatenate(rows, axis=0)
    high = part.astype(bf16)
    low = (part - high.astype(f32)).astype(bf16)
    at = 0
    for v in (tok, jnp.concatenate([high, low], axis=0)):
        for lo in range(0, t, m):
            pay_ref[at : at + v.shape[0], :] = v[:, lo : lo + m]
            at += v.shape[0]


def pack(tok_t, ag, au, fit):
    rank, d, m = ag.shape
    t = tok_t.shape[1]
    pay = (d + 4 * rank) * (t // m)
    return _call(
        _pack_kernel,
        "pack",
        flops=4 * rank * d * m * t,
        moved=8 * rank * d * m,
        in_specs=[FULL] * 4,
        out_specs=[FULL] * 3,
        out_shape=[jax.ShapeDtypeStruct((n, m), bf16) for n in (rank * d, rank * d, pay)],
    )(tok_t, ag, au, fit)


def _pick_kernel(y_ref, s_ref, pa_ref, pb_ref, out_ref):
    n = s_ref.shape[0]
    y = y_ref[0]
    for where, at, ref in (
        (y == 1, 0, pb_ref),
        (y == 2, 0, pa_ref),
        (jnp.logical_or(y == 0, y == 3), 0, s_ref),
        (y < 2, n, pa_ref),
        (y >= 2, n, pb_ref),
    ):

        @pl.when(where)
        def _():
            out_ref[at : at + n, :] = ref[...]


def pick(y, s, pa, pb):
    return _call(
        _pick_kernel,
        "pick",
        moved=8 * s.size,
        in_specs=[SCALARS, FULL, FULL, FULL],
        out_specs=FULL,
        out_shape=jax.ShapeDtypeStruct((2 * s.shape[0], s.shape[1]), s.dtype),
    )(y, s, pa, pb)


ORDER = (2, 1, 3, 0)


def _update_kernel(coeff, slabs, nb, nafter, block_ref, *refs):
    a_refs, b_refs = refs[:RING], refs[RING : RING + nb]
    pp_ref, pm_ref, rp_ref, rm_ref, own_ref, lhs_ref, rhs_ref = refs[RING + nb + nafter :]
    rank, q, m = b_refs[0].shape
    d = lhs_ref.shape[0]
    n = d // 2
    i = pl.program_id(0)

    @pl.when(i == 0)
    def _():
        for j, ref in enumerate(b_refs):
            row, col = (j % 2) * q, (j // 2) * rank * m
            for r in range(rank):
                rhs_ref[row : row + q, col + r * m : col + (r + 1) * m] = ref[r]

    for j, ref in enumerate(a_refs):

        @pl.when(block_ref[i] == j)
        def _():
            for k in range(slabs):
                lhs_ref[:, k * m : (k + 1) * m] = ref[k * d : (k + 1) * d, :]

    acc = lax.dot_general(lhs_ref[...], rhs_ref[...], NT, preferred_element_type=f32)
    acc = (acc * coeff).astype(bf16)

    @pl.when(i == 0)
    def _():
        pp_ref[:n, :] = acc[:n]
        pm_ref[:n, :] = acc[n:]

    @pl.when(i == 1)
    def _():
        pp_ref[n:, :] = acc[n:]
        rp_ref[...] = acc[:n]

    @pl.when(i == 2)
    def _():
        pm_ref[n:, :] = acc[:n]
        rm_ref[...] = acc[n:]

    @pl.when(i == 3)
    def _():
        own_ref[...] = acc


def update(coeff, block, factors, seconds, *after):
    rank, q, m = seconds[0].shape
    slabs = rank * len(seconds) // 2
    d = factors[0].shape[0] // slabs
    wide = 2 * q

    def once(shape):
        return pl.BlockSpec(shape, lambda i, w: (0,) * len(shape), pipeline_mode=pl.Buffered(1))

    def kept(n):
        return pl.BlockSpec((n, wide), lambda i, w: (0, 0))

    sizes = (d, d, d // 2, d // 2, d)
    return _call(
        functools.partial(_update_kernel, coeff, slabs, len(seconds), len(after)),
        "update",
        flops=2 * RING * d * slabs * m * wide,
        moved=2 * (RING * slabs * d * m + slabs * m * wide + RING * d * wide),
        grid_spec=pltpu.PrefetchScalarGridSpec(
            num_scalar_prefetch=1,
            grid=(RING,),
            in_specs=[once(f.shape) for f in factors] + [once(b.shape) for b in seconds] + _any(len(after)),
            out_specs=[kept(n) for n in sizes],
            scratch_shapes=[pltpu.VMEM((d, slabs * m), bf16), pltpu.VMEM((wide, slabs * m), bf16)],
        ),
        out_shape=[jax.ShapeDtypeStruct((n, wide), bf16) for n in sizes],
    )(block, *factors, *seconds, *after)


def over_z(pp, pm, rp, rm, own):
    n = rp.shape[0]
    gp, gm = swap(pp, "z", 1), swap(pm, "z", -1)
    fp = swap(rp + gp[:n], "z", 1)
    fm = swap(rm + gm[:n], "z", -1)
    own = own.astype(f32)
    first = own[:n] + gm[n:].astype(f32) + fp.astype(f32)
    second = own[n:] + gp[n:].astype(f32) + fm.astype(f32)
    return jnp.concatenate([first, second], axis=0)


def _tokens_kernel(at_ref, *refs):
    ins, (tok_ref, part_ref) = refs[:RING], refs[RING:]
    _, _, d, t = tok_ref.shape
    m = ins[0].shape[2]
    x, h = at_ref[0], at_ref[1]
    wide = t // m
    total = None
    for j, ref in enumerate(ins):
        for s in range(2):
            rows = [ref[s, i * d : (i + 1) * d, :] for i in range(wide)]
            tok_ref[lax.rem(x + RING - j, RING), h if s == 0 else 1 - h] = jnp.concatenate(rows, axis=1)
            last = ref[s, wide * d :, :].astype(f32)
            n = last.shape[0] // wide
            both = jnp.concatenate([last[i * n : (i + 1) * n] for i in range(wide)], axis=1)
            value = both[: n // 2] + both[n // 2 :]
            total = value if total is None else total + value
    part_ref[...] = total


def tokens_of(at, parts, d, t, probes):
    return _call(
        _tokens_kernel,
        "tokens",
        moved=16 * parts[0].size,
        in_specs=[SCALARS] + [FULL] * RING,
        out_specs=[FULL] * 2,
        out_shape=[jax.ShapeDtypeStruct((RING, 2, d, t), bf16), jax.ShapeDtypeStruct((probes, t), f32)],
    )(at, *parts)


def _hidden_kernel(c_ref, mine_ref, other_ref, p0_ref, p1_ref, wg_ref, wu_ref, bg_ref, bu_ref, *refs):
    out_ref, tok_ref, p_ref = refs[-3:]
    rank, _, m = bg_ref.shape
    nx, nh, d, t = mine_ref.shape

    @pl.when(pl.program_id(0) == 0)
    def _():
        c = c_ref[0]
        for ref, core in ((mine_ref, c), (other_ref, 1 - c)):
            for i in range(nx):
                for j in range(nh):
                    row = pl.multiple_of((2 * (nh * i + j) + core) * d, d)
                    tok_ref[pl.ds(row, d), :] = ref[i, j]
        mask = _own_mask(m, t)
        probe = (p0_ref[...] + p1_ref[...]).astype(bf16).astype(f32) * noise_scale
        for i in range(2 * rank):
            row = jnp.broadcast_to(probe[i : i + 1, :], (m, t))
            p_ref[i * m : (i + 1) * m, :] = jnp.where(mask, row, 0.0).astype(bf16)

    pre = []
    for k, (w_ref, b_ref) in enumerate(((wg_ref, bg_ref), (wu_ref, bu_ref))):
        b = jnp.concatenate([b_ref[r] for r in range(rank)], axis=1)
        acc = jnp.dot(w_ref[...], tok_ref[...], preferred_element_type=f32)
        acc += jnp.dot(b, p_ref[k * rank * m : (k + 1) * rank * m, :], preferred_element_type=f32)
        pre.append(acc)
    g, u = pre
    out_ref[...] = (g / (1.0 + jnp.exp(-g)) * u).astype(out_ref.dtype)


def hidden_of(c, mine, other, p0, p1, wg, wu, bg, bu, *after):
    t = mine.shape[3]
    q, d = wg.shape
    rank, _, m = bg.shape
    block = 304
    w_spec = pl.BlockSpec((block, d), lambda i: (i, 0))
    b_spec = pl.BlockSpec((rank, block, m), lambda i: (0, i, 0))
    t_spec = pl.BlockSpec(mine.shape, lambda i: (0, 0, 0, 0), pipeline_mode=pl.Buffered(1))
    p_spec = pl.BlockSpec(p0.shape, lambda i: (0, 0))
    return _call(
        _hidden_kernel,
        "hidden",
        flops=4 * q * t * (d + rank * m),
        moved=2 * (2 * q * d + d * t + 2 * rank * q * m + q * t),
        grid=(pl.cdiv(q, block),),
        in_specs=[SCALARS, t_spec, t_spec, p_spec, p_spec, w_spec, w_spec, b_spec, b_spec] + _any(len(after)),
        out_specs=pl.BlockSpec((block, t), lambda i: (i, 0)),
        out_shape=jax.ShapeDtypeStruct((q, t), bf16),
        scratch_shapes=[pltpu.VMEM((d, t), bf16), pltpu.VMEM((2 * rank * m, t), bf16)],
    )(c, mine, other, p0, p1, wg, wu, bg, bu, *after)


def local(tokens, w_gate, w_up, a_gate, a_up, b_gate, b_up, fitness):
    members, rank, d = a_gate.shape
    q = w_gate.shape[1]
    coeff = 1.0 / (members * lax.axis_size("z") * lax.axis_size("l") * rank) ** 0.5
    z, l, x, h, c = (lax.axis_index(a) for a in AXES)
    tok_t = tokens.T
    ag_t, au_t = (a.transpose(1, 2, 0) for a in (a_gate, a_up))
    bg, bu = (b.transpose(1, 2, 0) for b in (b_gate, b_up))
    block = (x - z - jnp.array(ORDER, jnp.int32)) % RING

    sg, su, pay = pack(tok_t, ag_t, au_t, fitness[None, :])
    bu_c, bg_c = swap(bu, "c"), swap(bg, "c")

    def round_x(v):
        return [v] + [swap(v, "x", k) for k in range(1, RING)]

    su_x = round_x(su)
    so_x = round_x(tie(swap(su, "h"), *su_x[1:]))
    at_y = (0, 2, 1, 3)
    pa, pb = (
        lax.ppermute(sg, ("l", "h"), [(at_y[i], at_y[j]) for i, j in pairs])
        for pairs in (((1, 0), (2, 1), (0, 2)), ((3, 1), (1, 2), (2, 3)))
    )
    both = pick((2 * h + l).reshape(1), sg, pa, pb)
    bg_far = swap(tie(bg, both), "l")
    bg_far_c = swap(bg_far, "c")
    sg_x = round_x(tie(both, *so_x[1:]))
    pays = tie(jnp.stack([pay, swap(pay, "h")]), *sg_x[1:])
    tok, part = tokens_of(jnp.stack([x, h]), round_x(pays), d, tok_t.shape[1], 2 * rank)

    ua = update(coeff, block, su_x, [bu, bu_c])
    ub = update(coeff, block, so_x, [bu, bu_c], ua[-1])
    gg = update(coeff, block, sg_x, [bg, bg_c, bg_far, bg_far_c], ub[-1])
    hidden = hidden_of(
        c.reshape(1), tok, swap(tok, "c"), part, swap(part, "c"), w_gate.T, w_up.T, bg, bu, gg[-1]
    ).T

    sum_a, sum_b = over_z(*ua), over_z(*ub)
    mine = l == h
    sent = swap(jnp.where(mine, sum_b, sum_a).astype(bf16), "l")
    up = jnp.where(mine, sum_a, sum_b) + sent.astype(f32)
    gate = over_z(*gg)

    rows = 2 * d
    first = (2 * z + l) * rows
    news = []
    for w, total in ((w_gate, gate), (w_up, up)):
        held = lax.dynamic_slice_in_dim(w, first, rows, 0).astype(f32)
        near, far = total[:, :q], swap(total[:, q:].astype(bf16), "c").astype(f32)
        both_rows = jnp.where(c == 0, jnp.concatenate([near, far]), jnp.concatenate([far, near]))
        news.append((held + both_rows).astype(bf16))
    return hidden, news[0], news[1]


def solution(mesh):
    fine = Mesh(mesh.devices.reshape(4, 2, 4, 2, 2), AXES)
    pop, mp = ("z", "l"), ("x", "h", "c")
    return jax.shard_map(
        local,
        mesh=fine,
        in_specs=(
            P(pop, mp),
            P(None, mp),
            P(None, mp),
            P(pop, None, mp),
            P(pop, None, mp),
            P(pop, None, mp),
            P(pop, None, mp),
            P(pop),
        ),
        out_specs=(P(pop, mp), P(pop, mp), P(pop, mp)),
        check_vma=False,
    )
```

```python
import functools

import jax
import jax.numpy as jnp
from jax import lax
from jax.experimental import pallas as pl
from jax.experimental.pallas import tpu as pltpu
from jax.sharding import Mesh
from jax.sharding import PartitionSpec as P

bf16 = jnp.bfloat16
f32 = jnp.float32
noise_scale = 0.5
AXES = ("z", "l", "x", "h", "c")
RING = 4
VMEM = 58 * 1024 * 1024
HINT = 1
NT = (((1,), (1,)), ((), ()))
TN = (((0,), (0,)), ((), ()))


def _call(kernel, name, flops=0, moved=0, **kw):
    return pl.pallas_call(
        kernel,
        name=name,
        compiler_params=pltpu.CompilerParams(vmem_limit_bytes=VMEM),
        cost_estimate=pl.CostEstimate(flops=flops // HINT, bytes_accessed=moved // HINT, transcendentals=0),
        **kw,
    )


def _any(n):
    return [pl.BlockSpec(memory_space=pl.ANY)] * n


FULL = pl.BlockSpec(memory_space=pltpu.VMEM)
SCALARS = pl.BlockSpec(memory_space=pltpu.SMEM)


def swap(v, axis, shift=1):
    n = lax.axis_size(axis)
    return lax.ppermute(v, axis, [(i, (i + shift) % n) for i in range(n)])


def join(vs, *after):
    n = len(vs)
    return _call(
        lambda *refs: None,
        "join",
        in_specs=_any(n + len(after)),
        out_specs=_any(n),
        out_shape=[jax.ShapeDtypeStruct(v.shape, v.dtype) for v in vs],
        input_output_aliases={i: i for i in range(n)},
    )(*vs, *after)


def tie(v, *after):
    return join([v], *after)[0]


def _own_mask(members, tokens):
    m = lax.broadcasted_iota(jnp.int32, (members, tokens), 0)
    t = lax.broadcasted_iota(jnp.int32, (members, tokens), 1)
    return jnp.logical_or(t == 2 * m, t == 2 * m + 1)


def _pack_kernel(tok_ref, ag_ref, au_ref, fit_ref, sg_ref, su_ref, all_ref):
    rank, d, m = ag_ref.shape
    tok = tok_ref[...]
    t = tok.shape[1]
    fit = fit_ref[...]
    mask = _own_mask(m, t)
    rows = []
    for a_ref, s_refs in ((ag_ref, (sg_ref,)), (au_ref, (su_ref, all_ref))):
        for r in range(rank):
            a = a_ref[r]
            for s_ref in s_refs:
                s_ref[r * d : (r + 1) * d, :] = (a.astype(f32) * fit).astype(bf16)
            s = lax.dot_general(a, tok, TN, preferred_element_type=f32)
            rows.append(jnp.sum(jnp.where(mask, s, 0.0), axis=0, keepdims=True))
    part = jnp.concatenate(rows, axis=0)
    high = part.astype(bf16)
    low = (part - high.astype(f32)).astype(bf16)
    at = rank * d
    for v in (tok, jnp.concatenate([high, low], axis=0)):
        for lo in range(0, t, m):
            all_ref[at : at + v.shape[0], :] = v[:, lo : lo + m]
            at += v.shape[0]


def pack(tok_t, ag, au, fit):
    rank, d, m = ag.shape
    t = tok_t.shape[1]
    pay = (d + 4 * rank) * (t // m)
    return _call(
        _pack_kernel,
        "pack",
        flops=4 * rank * d * m * t,
        moved=8 * rank * d * m,
        in_specs=[FULL] * 4,
        out_specs=[FULL] * 3,
        out_shape=[jax.ShapeDtypeStruct((n, m), bf16) for n in (rank * d, rank * d, rank * d + pay)],
    )(tok_t, ag, au, fit)


def _pick_kernel(y_ref, s_ref, pa_ref, pb_ref, all_ref, *refs):
    out_ref = refs[-1]
    n = s_ref.shape[0]
    y = y_ref[0]
    for where, at, ref in (
        (y == 1, 0, pb_ref),
        (y == 2, 0, pa_ref),
        (jnp.logical_or(y == 0, y == 3), 0, s_ref),
        (y < 2, n, pa_ref),
        (y >= 2, n, pb_ref),
    ):

        @pl.when(where)
        def _():
            out_ref[at : at + n, :] = ref[...]

    out_ref[2 * n :, :] = all_ref[n:, :]


def pick(y, s, pa, pb, rest, *after):
    n, m = s.shape
    return _call(
        _pick_kernel,
        "pick",
        moved=8 * s.size,
        in_specs=[SCALARS, FULL, FULL, FULL, FULL] + _any(len(after)),
        out_specs=FULL,
        out_shape=jax.ShapeDtypeStruct((n + rest.shape[0], m), s.dtype),
    )(y, s, pa, pb, rest, *after)


def rows_of(refs, lo, hi):
    if len(refs) == 1:
        return refs[0][lo:hi, :]
    n = refs[0].shape[0]
    parts = []
    if lo < n:
        parts.append(refs[0][lo : min(hi, n), :])
    if hi > n:
        parts.append(refs[1][max(lo, n) - n : hi - n, :])
    return parts[0] if len(parts) == 1 else jnp.concatenate(parts, axis=0)


def blocks_of(refs):
    own, one, two_lo, two_hi, three = refs
    return [own], [one], [two_lo, two_hi], [three]


PIECES = 5


ORDER = (2, 1, 3, 0)


def _update_kernel(coeff, slabs, d, rest, nb, nafter, block_ref, *refs):
    blocks = blocks_of(refs[:PIECES])
    b_refs = refs[PIECES : PIECES + nb]
    pp_ref, pm_ref, rp_ref, rm_ref, own_ref, lhs_ref = refs[PIECES + nb + nafter :]
    m = b_refs[0].shape[2]
    n = d // 2
    i = pl.program_id(0)

    @pl.when(i == 0)
    def _():
        for step in range(RING):
            for j, block in enumerate(blocks):

                @pl.when(block_ref[step] == j)
                def _():
                    for k in range(slabs):
                        lhs_ref[step * d : (step + 1) * d, k * m : (k + 1) * m] = rows_of(block, k * d, (k + 1) * d)

    def product(sides, rows):
        rhs = []
        for first in range(0, nb, 2):
            for r in range(b_refs[first].shape[0]):
                parts = [b_refs[first + side][r, :rows, :] for side in sides]
                rhs.append(parts[0] if len(parts) == 1 else jnp.concatenate(parts, axis=0))
        acc = lax.dot_general(lhs_ref[...], jnp.concatenate(rhs, axis=1), NT, preferred_element_type=f32)
        acc = (acc * coeff).astype(bf16)
        two, one, back, own = (acc[k * d : (k + 1) * d] for k in range(RING))
        w = acc.shape[1]
        pp_ref[:n, :w] = two[:n]
        pm_ref[:n, :w] = two[n:]
        pp_ref[n:, :w] = one[n:]
        rp_ref[:, :w] = one[:n]
        pm_ref[n:, :w] = back[:n]
        rm_ref[:, :w] = back[n:]
        own_ref[:, :w] = own

    size = b_refs[0].shape[1]

    @pl.when(i < 3)
    def _():
        product((0,), size)

    @pl.when(jnp.logical_and(i >= 3, i < 6))
    def _():
        product((1,), size)

    @pl.when(i == 6)
    def _():
        product((0, 1), rest)


CUT = 384


def update(coeff, block, rows, factors, seconds, *after):
    _, q, m = seconds[0].shape
    slabs = sum(b.shape[0] for b in seconds[::2])
    d = rows
    wide = 2 * q

    def once(shape):
        return pl.BlockSpec(shape, lambda i, w: (0,) * len(shape), pipeline_mode=pl.Buffered(1))

    def cut(n):
        return pl.BlockSpec((n, CUT), lambda i, w: (0, i))

    def near(b):
        return pl.BlockSpec((b.shape[0], CUT, m), lambda i, w: (0, jnp.minimum(i, 3), 0))

    def far(b):
        return pl.BlockSpec((b.shape[0], CUT, m), lambda i, w: (0, jnp.maximum(i - 3, 0), 0))

    sizes = (d, d, d // 2, d // 2, d)
    return _call(
        functools.partial(_update_kernel, coeff, slabs, d, q - 3 * CUT, len(seconds), len(after)),
        "update",
        flops=2 * RING * d * slabs * m * wide,
        moved=2 * (RING * slabs * d * m + slabs * m * wide + RING * d * wide),
        grid_spec=pltpu.PrefetchScalarGridSpec(
            num_scalar_prefetch=1,
            grid=(7,),
            in_specs=[once(f.shape) for f in factors] + [(near, far)[i % 2](b) for i, b in enumerate(seconds)] + _any(len(after)),
            out_specs=[cut(n) for n in sizes],
            scratch_shapes=[pltpu.VMEM((RING * d, slabs * m), bf16)],
        ),
        out_shape=[jax.ShapeDtypeStruct((n, wide), bf16) for n in sizes],
    )(block, *factors, *seconds, *after)


def _at(shape, row=0):
    return pl.BlockSpec(shape, lambda i: (row, 0))


def _relay_kernel(gp_ref, gm_ref, rp_ref, rm_ref, *refs):
    ap_ref, am_ref = refs[-2:]
    ap_ref[...] = (rp_ref[...].astype(f32) + gp_ref[...].astype(f32)).astype(bf16)
    am_ref[...] = (rm_ref[...].astype(f32) + gm_ref[...].astype(f32)).astype(bf16)


def relay(gp, gm, rp, rm, *after):
    spec = _at(rp.shape)
    return _call(
        _relay_kernel,
        "relay",
        grid=(1,),
        moved=12 * rp.size,
        in_specs=[spec] * 4 + _any(len(after)),
        out_specs=[spec] * 2,
        out_shape=[jax.ShapeDtypeStruct(rp.shape, bf16)] * 2,
    )(gp, gm, rp, rm, *after)


def _halves_kernel(one_ref, three_ref, *refs):
    lo_ref, hi_ref = refs[-2:]
    lo_ref[...] = one_ref[...]
    hi_ref[...] = three_ref[...]


def halves(one, three, *after):
    n, m = one.shape[0] // 2, one.shape[1]
    return _call(
        _halves_kernel,
        "halves",
        grid=(1,),
        moved=8 * n * m,
        in_specs=[_at((n, m)), _at((n, m), 1)] + _any(len(after)),
        out_specs=[_at((n, m))] * 2,
        out_shape=[jax.ShapeDtypeStruct((n, m), bf16)] * 2,
    )(one, three, *after)


def _total(own_ref, gp_ref, gm_ref, fp_ref, fm_ref):
    n = fp_ref.shape[0]
    first = own_ref[:n, :].astype(f32) + gm_ref[n:, :].astype(f32) + fp_ref[...].astype(f32)
    second = own_ref[n:, :].astype(f32) + gp_ref[n:, :].astype(f32) + fm_ref[...].astype(f32)
    return jnp.concatenate([first, second], axis=0)


def _split(total, near_ref, far_ref):
    q, k = near_ref.shape[1], 3 * CUT
    near_ref[:, :k] = total[:, :k]
    near_ref[:, k:] = total[:, 2 * k : k + q]
    far_ref[:, :k] = total[:, k : 2 * k].astype(bf16)
    far_ref[:, k:] = total[:, k + q :].astype(bf16)


def _ends(shape):
    d, q = shape[0], shape[1] // 2
    return [jax.ShapeDtypeStruct((d, q), f32), jax.ShapeDtypeStruct((d, q), bf16)]


def gate_sum(*parts):
    def kernel(*refs):
        _split(_total(*refs[:5]), *refs[5:])

    return _call(
        kernel,
        "gate_sum",
        moved=14 * parts[0].size,
        in_specs=[FULL] * 5,
        out_specs=[FULL] * 2,
        out_shape=_ends(parts[0].shape),
    )(*parts)


def _up_sums_kernel(mine_ref, *refs):
    keep_ref, send_ref = refs[10:]
    a, b = _total(*refs[:5]), _total(*refs[5:10])
    mine = mine_ref[0] == 1
    keep_ref[...] = jnp.where(mine, a, b)
    send_ref[...] = jnp.where(mine, b, a).astype(bf16)


def up_sums(mine, parts_a, parts_b, *after):
    shape = parts_a[0].shape

    def kernel(mine_ref, *refs):
        _up_sums_kernel(mine_ref, *refs[:10], *refs[-2:])

    return _call(
        kernel,
        "up_sums",
        moved=28 * parts_a[0].size,
        in_specs=[SCALARS] + [FULL] * 10 + _any(len(after)),
        out_specs=[FULL] * 2,
        out_shape=[jax.ShapeDtypeStruct(shape, f32), jax.ShapeDtypeStruct(shape, bf16)],
    )(mine, *parts_a, *parts_b, *after)


def up_sum(keep, sent):
    def kernel(keep_ref, sent_ref, near_ref, far_ref):
        _split(keep_ref[...] + sent_ref[...].astype(f32), near_ref, far_ref)

    return _call(
        kernel,
        "up_sum",
        moved=12 * keep.size,
        in_specs=[FULL] * 2,
        out_specs=[FULL] * 2,
        out_shape=_ends(keep.shape),
    )(keep, sent)


def _renew_kernel(c_ref, held_ref, near_ref, far_ref, out_ref):
    d = near_ref.shape[0]
    near, far = near_ref[...], far_ref[...].astype(f32)

    def put(first, second):
        out_ref[:d, :] = (held_ref[:d, :].astype(f32) + first).astype(bf16)
        out_ref[d:, :] = (held_ref[d:, :].astype(f32) + second).astype(bf16)

    @pl.when(c_ref[0] == 0)
    def _():
        put(near, far)

    @pl.when(c_ref[0] == 1)
    def _():
        put(far, near)


def renew(c, held, near, far):
    return _call(
        _renew_kernel,
        "renew",
        moved=6 * held.size,
        in_specs=[SCALARS] + [FULL] * 3,
        out_specs=FULL,
        out_shape=jax.ShapeDtypeStruct(held.shape, bf16),
    )(c, held, near, far)


def _tokens_kernel(n, at_ref, *refs):
    tok_ref = refs[-1]
    t, m = tok_ref.shape[1], refs[0].shape[1]
    d = (tok_ref.shape[0] - 2 * n) // (2 * RING)
    x, h = at_ref[0], at_ref[1]
    wide = t // m
    total = None
    for s in range(2):
        gather = refs[s * PIECES : (s + 1) * PIECES]
        start = gather[0].shape[0] - wide * (d + 2 * n)
        for j, block in enumerate(blocks_of(gather)):
            rows = [rows_of(block, start + i * d, start + (i + 1) * d) for i in range(wide)]
            to = 2 * lax.rem(x + RING - j, RING) + (h if s == 0 else 1 - h)
            tok_ref[pl.ds(pl.multiple_of(to * d, d), d), :] = jnp.concatenate(rows, axis=1)
            at = start + wide * d
            terms = [rows_of(block, at + i * 2 * n, at + (i + 1) * 2 * n).astype(f32) for i in range(wide)]
            both = jnp.concatenate(terms, axis=1)
            value = both[:n] + both[n:]
            total = value if total is None else total + value
    high = total.astype(bf16)
    low = (total - high.astype(f32)).astype(bf16)
    tok_ref[2 * RING * d :, :] = jnp.concatenate([high, low], axis=0)


def tokens_of(at, own, other, d, t, probes, *after):
    return _call(
        functools.partial(_tokens_kernel, probes),
        "tokens",
        moved=8 * RING * 2 * d * t,
        in_specs=[SCALARS] + [FULL] * (2 * PIECES) + _any(len(after)),
        out_specs=FULL,
        out_shape=jax.ShapeDtypeStruct((2 * RING * d + 2 * probes, t), bf16),
    )(at, *own, *other, *after)


def _hidden_kernel(c_ref, mine_ref, other_ref, wg_ref, wu_ref, bg_ref, bu_ref, *refs):
    out_ref, tok_ref, p_ref = refs[-3:]
    rank, _, m = bg_ref.shape
    t = mine_ref.shape[1]
    n = 2 * rank
    d = (mine_ref.shape[0] - 2 * n) // (2 * RING)

    @pl.when(pl.program_id(0) == 0)
    def _():
        c = c_ref[0]
        for ref, core in ((mine_ref, c), (other_ref, 1 - c)):
            for i in range(2 * RING):
                tok_ref[pl.ds(pl.multiple_of((2 * i + core) * d, d), d), :] = ref[i * d : (i + 1) * d, :]
        mask = _own_mask(m, t)
        terms = mine_ref[2 * RING * d :, :].astype(f32) + other_ref[2 * RING * d :, :].astype(f32)
        probe = (terms[:n] + terms[n:]).astype(bf16).astype(f32) * noise_scale
        for i in range(2 * rank):
            row = jnp.broadcast_to(probe[i : i + 1, :], (m, t))
            p_ref[i * m : (i + 1) * m, :] = jnp.where(mask, row, 0.0).astype(bf16)

    pre = []
    for k, (w_ref, b_ref) in enumerate(((wg_ref, bg_ref), (wu_ref, bu_ref))):
        b = jnp.concatenate([b_ref[r] for r in range(rank)], axis=1)
        acc = jnp.dot(w_ref[...], tok_ref[...], preferred_element_type=f32)
        acc += jnp.dot(b, p_ref[k * rank * m : (k + 1) * rank * m, :], preferred_element_type=f32)
        pre.append(acc)
    g, u = pre
    out_ref[...] = (g / (1.0 + jnp.exp(-g)) * u).astype(out_ref.dtype)


def hidden_of(c, mine, other, wg, wu, bg, bu, *after):
    t = mine.shape[1]
    q, d = wg.shape
    rank, _, m = bg.shape
    block = 304
    w_spec = pl.BlockSpec((block, d), lambda i: (i, 0))
    b_spec = pl.BlockSpec((rank, block, m), lambda i: (0, i, 0))
    t_spec = pl.BlockSpec(mine.shape, lambda i: (0, 0), pipeline_mode=pl.Buffered(1))
    return _call(
        _hidden_kernel,
        "hidden",
        flops=4 * q * t * (d + rank * m),
        moved=2 * (2 * q * d + d * t + 2 * rank * q * m + q * t),
        grid=(pl.cdiv(q, block),),
        in_specs=[SCALARS, t_spec, t_spec, w_spec, w_spec, b_spec, b_spec] + _any(len(after)),
        out_specs=pl.BlockSpec((block, t), lambda i: (i, 0)),
        out_shape=jax.ShapeDtypeStruct((q, t), bf16),
        scratch_shapes=[pltpu.VMEM((d, t), bf16), pltpu.VMEM((2 * rank * m, t), bf16)],
    )(c, mine, other, wg, wu, bg, bu, *after)


def local(tokens, w_gate, w_up, a_gate, a_up, b_gate, b_up, fitness):
    members, rank, d = a_gate.shape
    q = w_gate.shape[1]
    coeff = 1.0 / (members * lax.axis_size("z") * lax.axis_size("l") * rank) ** 0.5
    z, l, x, h, c = (lax.axis_index(a) for a in AXES)
    tok_t = tokens.T
    ag_t, au_t = (a.transpose(1, 2, 0) for a in (a_gate, a_up))
    bg, bu = (b.transpose(1, 2, 0) for b in (b_gate, b_up))
    block = (x - z - jnp.array(ORDER, jnp.int32)) % RING

    sg, su, rest = pack(tok_t, ag_t, au_t, fitness[None, :])
    bu_c = swap(bu, "c")

    def hop(axis, first, second):
        return swap(first, axis, 1), swap(second, axis, -1)

    one, three = hop("x", su, su)
    so = swap(rest, "h")
    first = (2 * z + l) * 2 * d
    held = [lax.dynamic_slice_in_dim(w, first, 2 * d, 0) for w in (w_gate, w_up)]
    one, three, bu_c, *held = join([one, three, bu_c, *held])
    at_y = (0, 2, 1, 3)
    sg_y = tie(sg, so)
    pa, pb = (
        lax.ppermute(sg_y, ("l", "h"), [(at_y[i], at_y[j]) for i, j in pairs])
        for pairs in (((1, 0), (2, 1), (0, 2)), ((3, 1), (1, 2), (2, 3)))
    )
    lo, hi, so = join([*hop("x", *halves(one, three)), so])
    su_x = (su, one, lo, hi, three)
    so = tie(so, lo)
    one, three = hop("x", so, so)
    ua = update(coeff, block, d, su_x, [bu, bu_c], so)
    gp_a, gm_a = hop("z", *ua[:2])
    one, three = join([one, three], ua[-1])
    lo, hi = hop("x", *halves(one, three))
    both = pick((2 * h + l).reshape(1), sg_y, pa, pb, rest, one)
    far_0 = swap(tie(bg, both), "l")
    lo, hi = join([lo, hi], both)
    so_x = (so, one, lo, hi, three)
    both = tie(both, lo)
    one, three = hop("x", both, both)
    ub = update(coeff, block, d, so_x, [bu, bu_c], both)
    gp_a, gm_a = join([gp_a, gm_a], ub[-1])
    ap, am = relay(gp_a, gm_a, *ua[2:4])
    fp_a, fm_a = hop("z", ap, am)
    one, three = join([one, three], ap, ub[-1])
    lo, hi = hop("x", *halves(one, three))
    fp_a, fm_a = join([fp_a, fm_a], one)
    gp_b, gm_b = hop("z", *join(ub[:2], fp_a))
    lo, hi = join([lo, hi], fp_a)
    sg_x = (both, one, lo, hi, three)
    bg_c = swap(tie(bg, lo), "c")
    tok = tokens_of(jnp.stack([x, h]), sg_x, so_x, d, tok_t.shape[1], 2 * rank)
    tok_c = swap(tok, "c")
    gp_b, gm_b, far_0 = join([gp_b, gm_b, far_0], tok)
    ap, am = relay(gp_b, gm_b, *ub[2:4])
    fp_b, fm_b = hop("z", ap, am)
    fars = [v for far in (far_0,) for v in (far, swap(far, "c"))]
    gg = update(coeff, block, d, sg_x, [bg, bg_c, *fars], ap)
    fp_b, fm_b = join([fp_b, fm_b], gg[-1])
    gp_g, gm_g = hop("z", *gg[:2])
    keep, send = up_sums(
        (l == h).astype(jnp.int32).reshape(1), (ua[4], gp_a, gm_a, fp_a, fm_a), (ub[4], gp_b, gm_b, fp_b, fm_b)
    )
    sent = swap(send, "l")
    hidden = hidden_of(c.reshape(1), tok, tok_c, w_gate.T, w_up.T, bg, bu, gg[-1])
    gp_g, gm_g = join([gp_g, gm_g], hidden)
    fp_g, fm_g = hop("z", *relay(gp_g, gm_g, *gg[2:4]))
    up_near, up_far = up_sum(keep, tie(sent, gp_g))
    fp_g, fm_g = join([fp_g, fm_g], up_near)
    gate_near, gate_far = gate_sum(gg[4], gp_g, gm_g, fp_g, fm_g)

    news = [
        renew(c.reshape(1), w, near, swap(far, "c"))
        for w, near, far in ((held[0], gate_near, gate_far), (held[1], up_near, up_far))
    ]
    return hidden.T, news[0], news[1]


def solution(mesh):
    fine = Mesh(mesh.devices.reshape(4, 2, 4, 2, 2), AXES)
    pop, mp = ("z", "l"), ("x", "h", "c")
    return jax.shard_map(
        local,
        mesh=fine,
        in_specs=(
            P(pop, mp),
            P(None, mp),
            P(None, mp),
            P(pop, None, mp),
            P(pop, None, mp),
            P(pop, None, mp),
            P(pop, None, mp),
            P(pop),
        ),
        out_specs=(P(pop, mp), P(pop, mp), P(pop, mp)),
        check_vma=False,
    )
```

```python
import functools

import jax
import jax.numpy as jnp
from jax import lax
from jax.experimental import pallas as pl
from jax.experimental.pallas import tpu as pltpu
from jax.sharding import Mesh
from jax.sharding import PartitionSpec as P

bf16 = jnp.bfloat16
f32 = jnp.float32
noise_scale = 0.5
AXES = ("z", "l", "x", "h", "c")
RING = 4
VMEM = 58 * 1024 * 1024
HINT = 1
NT = (((1,), (1,)), ((), ()))
TN = (((0,), (0,)), ((), ()))


def _call(kernel, name, flops=0, moved=0, **kw):
    return pl.pallas_call(
        kernel,
        name=name,
        compiler_params=pltpu.CompilerParams(vmem_limit_bytes=VMEM),
        cost_estimate=pl.CostEstimate(flops=flops // HINT, bytes_accessed=moved // HINT, transcendentals=0),
        **kw,
    )


def _any(n):
    return [pl.BlockSpec(memory_space=pl.ANY)] * n


FULL = pl.BlockSpec(memory_space=pltpu.VMEM)
SCALARS = pl.BlockSpec(memory_space=pltpu.SMEM)


def swap(v, axis, shift=1):
    n = lax.axis_size(axis)
    return lax.ppermute(v, axis, [(i, (i + shift) % n) for i in range(n)])


def join(vs, *after):
    n = len(vs)
    return _call(
        lambda *refs: None,
        "join",
        in_specs=_any(n + len(after)),
        out_specs=_any(n),
        out_shape=[jax.ShapeDtypeStruct(v.shape, v.dtype) for v in vs],
        input_output_aliases={i: i for i in range(n)},
    )(*vs, *after)


def tie(v, *after):
    return join([v], *after)[0]


def _own_mask(members, tokens):
    m = lax.broadcasted_iota(jnp.int32, (members, tokens), 0)
    t = lax.broadcasted_iota(jnp.int32, (members, tokens), 1)
    return jnp.logical_or(t == 2 * m, t == 2 * m + 1)


def _pack_kernel(tok_ref, ag_ref, au_ref, fit_ref, sg_ref, su_ref, all_ref):
    rank, d, m = ag_ref.shape
    tok = tok_ref[...]
    t = tok.shape[1]
    fit = fit_ref[...]
    mask = _own_mask(m, t)
    rows = []
    for a_ref, s_refs in ((ag_ref, (sg_ref,)), (au_ref, (su_ref, all_ref))):
        for r in range(rank):
            a = a_ref[r]
            for s_ref in s_refs:
                s_ref[r * d : (r + 1) * d, :] = (a.astype(f32) * fit).astype(bf16)
            s = lax.dot_general(a, tok, TN, preferred_element_type=f32)
            rows.append(jnp.sum(jnp.where(mask, s, 0.0), axis=0, keepdims=True))
    part = jnp.concatenate(rows, axis=0)
    high = part.astype(bf16)
    low = (part - high.astype(f32)).astype(bf16)
    at = rank * d
    for v in (tok, jnp.concatenate([high, low], axis=0)):
        for lo in range(0, t, m):
            all_ref[at : at + v.shape[0], :] = v[:, lo : lo + m]
            at += v.shape[0]


def pack(tok_t, ag, au, fit):
    rank, d, m = ag.shape
    t = tok_t.shape[1]
    pay = (d + 4 * rank) * (t // m)
    return _call(
        _pack_kernel,
        "pack",
        flops=4 * rank * d * m * t,
        moved=8 * rank * d * m,
        in_specs=[FULL] * 4,
        out_specs=[FULL] * 3,
        out_shape=[jax.ShapeDtypeStruct((n, m), bf16) for n in (rank * d, rank * d, rank * d + pay)],
    )(tok_t, ag, au, fit)


def _pick_kernel(y_ref, s_ref, pa_ref, pb_ref, all_ref, *refs):
    out_ref = refs[-1]
    n = s_ref.shape[0]
    y = y_ref[0]
    for where, at, ref in (
        (y == 1, 0, pb_ref),
        (y == 2, 0, pa_ref),
        (jnp.logical_or(y == 0, y == 3), 0, s_ref),
        (y < 2, n, pa_ref),
        (y >= 2, n, pb_ref),
    ):

        @pl.when(where)
        def _():
            out_ref[at : at + n, :] = ref[...]

    out_ref[2 * n :, :] = all_ref[n:, :]


def pick(y, s, pa, pb, rest, *after):
    n, m = s.shape
    return _call(
        _pick_kernel,
        "pick",
        moved=8 * s.size,
        in_specs=[SCALARS, FULL, FULL, FULL, FULL] + _any(len(after)),
        out_specs=FULL,
        out_shape=jax.ShapeDtypeStruct((n + rest.shape[0], m), s.dtype),
    )(y, s, pa, pb, rest, *after)


def rows_of(refs, lo, hi):
    if len(refs) == 1:
        return refs[0][lo:hi, :]
    n = refs[0].shape[0]
    parts = []
    if lo < n:
        parts.append(refs[0][lo : min(hi, n), :])
    if hi > n:
        parts.append(refs[1][max(lo, n) - n : hi - n, :])
    return parts[0] if len(parts) == 1 else jnp.concatenate(parts, axis=0)


def blocks_of(refs):
    own, one, two_lo, two_hi, three = refs
    return [own], [one], [two_lo, two_hi], [three]


PIECES = 5


ORDER = (2, 1, 3, 0)


def _update_kernel(coeff, slabs, d, rest, nb, nafter, block_ref, *refs):
    blocks = blocks_of(refs[:PIECES])
    b_refs = refs[PIECES : PIECES + nb]
    pp_ref, pm_ref, rp_ref, rm_ref, own_ref, lhs_ref = refs[PIECES + nb + nafter :]
    m = b_refs[0].shape[2]
    n = d // 2
    i = pl.program_id(0)

    @pl.when(i == 0)
    def _():
        for step in range(RING):
            for j, block in enumerate(blocks):

                @pl.when(block_ref[step] == j)
                def _():
                    for k in range(slabs):
                        lhs_ref[step * d : (step + 1) * d, k * m : (k + 1) * m] = rows_of(block, k * d, (k + 1) * d)

    def product(sides, rows):
        rhs = []
        for first in range(0, nb, 2):
            for r in range(b_refs[first].shape[0]):
                parts = [b_refs[first + side][r, :rows, :] for side in sides]
                rhs.append(parts[0] if len(parts) == 1 else jnp.concatenate(parts, axis=0))
        acc = lax.dot_general(lhs_ref[...], jnp.concatenate(rhs, axis=1), NT, preferred_element_type=f32)
        acc = (acc * coeff).astype(bf16)
        two, one, back, own = (acc[k * d : (k + 1) * d] for k in range(RING))
        w = acc.shape[1]
        pp_ref[:n, :w] = two[:n]
        pm_ref[:n, :w] = two[n:]
        pp_ref[n:, :w] = one[n:]
        rp_ref[:, :w] = one[:n]
        pm_ref[n:, :w] = back[:n]
        rm_ref[:, :w] = back[n:]
        own_ref[:, :w] = own

    size = b_refs[0].shape[1]

    @pl.when(i == 0)
    def _():
        product((0,), size)

    @pl.when(i == 1)
    def _():
        product((1,), size)

    @pl.when(i == 2)
    def _():
        product((0, 1), rest)


CUT = 1152


def update(coeff, block, rows, factors, seconds, *after):
    _, q, m = seconds[0].shape
    slabs = sum(b.shape[0] for b in seconds[::2])
    d = rows
    wide = 2 * q

    def once(shape):
        return pl.BlockSpec(shape, lambda i, w: (0,) * len(shape), pipeline_mode=pl.Buffered(1))

    def cut(n):
        return pl.BlockSpec((n, CUT), lambda i, w: (0, i))

    def near(b):
        return pl.BlockSpec((b.shape[0], CUT, m), lambda i, w: (0, jnp.minimum(i, 1), 0))

    def far(b):
        return pl.BlockSpec((b.shape[0], CUT, m), lambda i, w: (0, jnp.maximum(i - 1, 0), 0))

    sizes = (d, d, d // 2, d // 2, d)
    return _call(
        functools.partial(_update_kernel, coeff, slabs, d, q - CUT, len(seconds), len(after)),
        "update",
        flops=2 * RING * d * slabs * m * wide,
        moved=2 * (RING * slabs * d * m + slabs * m * wide + RING * d * wide),
        grid_spec=pltpu.PrefetchScalarGridSpec(
            num_scalar_prefetch=1,
            grid=(3,),
            in_specs=[once(f.shape) for f in factors] + [(near, far)[i % 2](b) for i, b in enumerate(seconds)] + _any(len(after)),
            out_specs=[cut(n) for n in sizes],
            scratch_shapes=[pltpu.VMEM((RING * d, slabs * m), bf16)],
        ),
        out_shape=[jax.ShapeDtypeStruct((n, wide), bf16) for n in sizes],
    )(block, *factors, *seconds, *after)


def _at(shape, row=0):
    return pl.BlockSpec(shape, lambda i: (row, 0))


def _relay_kernel(gp_ref, gm_ref, rp_ref, rm_ref, *refs):
    ap_ref, am_ref = refs[-2:]
    ap_ref[...] = (rp_ref[...].astype(f32) + gp_ref[...].astype(f32)).astype(bf16)
    am_ref[...] = (rm_ref[...].astype(f32) + gm_ref[...].astype(f32)).astype(bf16)


def relay(gp, gm, rp, rm, *after):
    spec = _at(rp.shape)
    return _call(
        _relay_kernel,
        "relay",
        grid=(1,),
        moved=12 * rp.size,
        in_specs=[spec] * 4 + _any(len(after)),
        out_specs=[spec] * 2,
        out_shape=[jax.ShapeDtypeStruct(rp.shape, bf16)] * 2,
    )(gp, gm, rp, rm, *after)


def _halves_kernel(one_ref, three_ref, *refs):
    lo_ref, hi_ref = refs[-2:]
    lo_ref[...] = one_ref[...]
    hi_ref[...] = three_ref[...]


def halves(one, three, *after):
    n, m = one.shape[0] // 2, one.shape[1]
    return _call(
        _halves_kernel,
        "halves",
        grid=(1,),
        moved=8 * n * m,
        in_specs=[_at((n, m)), _at((n, m), 1)] + _any(len(after)),
        out_specs=[_at((n, m))] * 2,
        out_shape=[jax.ShapeDtypeStruct((n, m), bf16)] * 2,
    )(one, three, *after)


def _total(own_ref, gp_ref, gm_ref, fp_ref, fm_ref):
    n = fp_ref.shape[0]
    first = own_ref[:n, :].astype(f32) + gm_ref[n:, :].astype(f32) + fp_ref[...].astype(f32)
    second = own_ref[n:, :].astype(f32) + gp_ref[n:, :].astype(f32) + fm_ref[...].astype(f32)
    return jnp.concatenate([first, second], axis=0)


def _split(total, near_ref, far_ref):
    q, k = near_ref.shape[1], CUT
    near_ref[:, :k] = total[:, :k]
    near_ref[:, k:] = total[:, 2 * k : k + q]
    far_ref[:, :k] = total[:, k : 2 * k].astype(far_ref.dtype)
    far_ref[:, k:] = total[:, k + q :].astype(far_ref.dtype)


def _ends(shape):
    d, q = shape[0], shape[1] // 2
    return [jax.ShapeDtypeStruct((d, q), f32), jax.ShapeDtypeStruct((d, q), bf16)]


def _gate_early_kernel(c_ref, held_ref, own_ref, gp_ref, gm_ref, *refs):
    near_ref, far_ref = refs[-2:]
    d = own_ref.shape[0]
    n = d // 2
    first = own_ref[:n, :].astype(f32) + gm_ref[n:, :].astype(f32)
    second = own_ref[n:, :].astype(f32) + gp_ref[n:, :].astype(f32)
    _split(jnp.concatenate([first, second], axis=0), near_ref, far_ref)
    near_ref[...] += held_ref[pl.ds(pl.multiple_of(c_ref[0] * d, d), d), :].astype(f32)


def gate_early(c, held, own, gp, gm, *after):
    d, q = own.shape[0], own.shape[1] // 2
    return _call(
        _gate_early_kernel,
        "gate_early",
        in_specs=[SCALARS] + [FULL] * 4 + _any(len(after)),
        out_specs=[FULL] * 2,
        out_shape=[jax.ShapeDtypeStruct((d, q), f32)] * 2,
    )(c, held, own, gp, gm, *after)


def _gate_late_kernel(near_ref, far_ref, fp_ref, fm_ref, out_ref, send_ref):
    n = fp_ref.shape[0]
    q, k = near_ref.shape[1], CUT
    for ref, rows in ((fp_ref, slice(0, n)), (fm_ref, slice(n, 2 * n))):
        out_ref[rows, :k] = (near_ref[rows, :k] + ref[:, :k].astype(f32)).astype(bf16)
        out_ref[rows, k:] = (near_ref[rows, k:] + ref[:, 2 * k : k + q].astype(f32)).astype(bf16)
        send_ref[rows, :k] = (far_ref[rows, :k] + ref[:, k : 2 * k].astype(f32)).astype(bf16)
        send_ref[rows, k:] = (far_ref[rows, k:] + ref[:, k + q :].astype(f32)).astype(bf16)


def gate_late(near, far, fp, fm):
    return _call(
        _gate_late_kernel,
        "gate_late",
        in_specs=[FULL] * 4,
        out_specs=[FULL] * 2,
        out_shape=[jax.ShapeDtypeStruct(near.shape, bf16)] * 2,
    )(near, far, fp, fm)


def _gate_rows_kernel(c_ref, held_ref, near_ref, far_ref, out_ref):
    d = near_ref.shape[0]
    c = c_ref[0]
    mine, other = pl.ds(pl.multiple_of(c * d, d), d), pl.ds(pl.multiple_of((1 - c) * d, d), d)
    out_ref[mine, :] = near_ref[...]
    out_ref[other, :] = (held_ref[other, :].astype(f32) + far_ref[...].astype(f32)).astype(bf16)


def gate_rows(c, held, near, far):
    return _call(
        _gate_rows_kernel,
        "gate_rows",
        in_specs=[SCALARS] + [FULL] * 3,
        out_specs=FULL,
        out_shape=jax.ShapeDtypeStruct(held.shape, bf16),
    )(c, held, near, far)


def _up_sums_kernel(mine_ref, *refs):
    keep_ref, send_ref = refs[10:]
    a, b = _total(*refs[:5]), _total(*refs[5:10])
    mine = mine_ref[0] == 1
    keep_ref[...] = jnp.where(mine, a, b)
    send_ref[...] = jnp.where(mine, b, a).astype(bf16)


def up_sums(mine, parts_a, parts_b, *after):
    shape = parts_a[0].shape

    def kernel(mine_ref, *refs):
        _up_sums_kernel(mine_ref, *refs[:10], *refs[-2:])

    return _call(
        kernel,
        "up_sums",
        in_specs=[SCALARS] + [FULL] * 10 + _any(len(after)),
        out_specs=[FULL] * 2,
        out_shape=[jax.ShapeDtypeStruct(shape, f32), jax.ShapeDtypeStruct(shape, bf16)],
    )(mine, *parts_a, *parts_b, *after)


def up_sum(keep, sent):
    def kernel(keep_ref, sent_ref, near_ref, far_ref):
        _split(keep_ref[...] + sent_ref[...].astype(f32), near_ref, far_ref)

    return _call(
        kernel,
        "up_sum",
        in_specs=[FULL] * 2,
        out_specs=[FULL] * 2,
        out_shape=_ends(keep.shape),
    )(keep, sent)


def _renew_kernel(c_ref, held_ref, near_ref, far_ref, out_ref):
    d = near_ref.shape[0]
    near, far = near_ref[...], far_ref[...].astype(f32)

    def put(first, second):
        out_ref[:d, :] = (held_ref[:d, :].astype(f32) + first).astype(bf16)
        out_ref[d:, :] = (held_ref[d:, :].astype(f32) + second).astype(bf16)

    @pl.when(c_ref[0] == 0)
    def _():
        put(near, far)

    @pl.when(c_ref[0] == 1)
    def _():
        put(far, near)


def renew(c, held, near, far):
    return _call(
        _renew_kernel,
        "renew",
        in_specs=[SCALARS] + [FULL] * 3,
        out_specs=FULL,
        out_shape=jax.ShapeDtypeStruct(held.shape, bf16),
    )(c, held, near, far)


def _tokens_kernel(n, at_ref, *refs):
    tok_ref = refs[-1]
    t, m = tok_ref.shape[1], refs[0].shape[1]
    d = (tok_ref.shape[0] - 2 * n) // (2 * RING)
    x, h = at_ref[0], at_ref[1]
    wide = t // m
    total = None
    for s in range(2):
        gather = refs[s * PIECES : (s + 1) * PIECES]
        start = gather[0].shape[0] - wide * (d + 2 * n)
        for j, block in enumerate(blocks_of(gather)):
            rows = [rows_of(block, start + i * d, start + (i + 1) * d) for i in range(wide)]
            to = 2 * lax.rem(x + RING - j, RING) + (h if s == 0 else 1 - h)
            tok_ref[pl.ds(pl.multiple_of(to * d, d), d), :] = jnp.concatenate(rows, axis=1)
            at = start + wide * d
            terms = [rows_of(block, at + i * 2 * n, at + (i + 1) * 2 * n).astype(f32) for i in range(wide)]
            both = jnp.concatenate(terms, axis=1)
            value = both[:n] + both[n:]
            total = value if total is None else total + value
    high = total.astype(bf16)
    low = (total - high.astype(f32)).astype(bf16)
    tok_ref[2 * RING * d :, :] = jnp.concatenate([high, low], axis=0)


def tokens_of(at, own, other, d, t, probes, *after):
    return _call(
        functools.partial(_tokens_kernel, probes),
        "tokens",
        moved=8 * RING * 2 * d * t,
        in_specs=[SCALARS] + [FULL] * (2 * PIECES) + _any(len(after)),
        out_specs=FULL,
        out_shape=jax.ShapeDtypeStruct((2 * RING * d + 2 * probes, t), bf16),
    )(at, *own, *other, *after)


def _hidden_kernel(c_ref, mine_ref, other_ref, wg_ref, wu_ref, bg_ref, bu_ref, *refs):
    out_ref, tok_ref, p_ref = refs[-3:]
    rank, _, m = bg_ref.shape
    t = mine_ref.shape[1]
    n = 2 * rank
    d = (mine_ref.shape[0] - 2 * n) // (2 * RING)

    @pl.when(pl.program_id(0) == 0)
    def _():
        c = c_ref[0]
        for ref, core in ((mine_ref, c), (other_ref, 1 - c)):
            for i in range(2 * RING):
                tok_ref[pl.ds(pl.multiple_of((2 * i + core) * d, d), d), :] = ref[i * d : (i + 1) * d, :]
        mask = _own_mask(m, t)
        terms = mine_ref[2 * RING * d :, :].astype(f32) + other_ref[2 * RING * d :, :].astype(f32)
        probe = (terms[:n] + terms[n:]).astype(bf16).astype(f32) * noise_scale
        for i in range(2 * rank):
            row = jnp.broadcast_to(probe[i : i + 1, :], (m, t))
            p_ref[i * m : (i + 1) * m, :] = jnp.where(mask, row, 0.0).astype(bf16)

    pre = []
    for k, (w_ref, b_ref) in enumerate(((wg_ref, bg_ref), (wu_ref, bu_ref))):
        b = jnp.concatenate([b_ref[r] for r in range(rank)], axis=1)
        acc = jnp.dot(w_ref[...], tok_ref[...], preferred_element_type=f32)
        acc += jnp.dot(b, p_ref[k * rank * m : (k + 1) * rank * m, :], preferred_element_type=f32)
        pre.append(acc)
    g, u = pre
    out_ref[...] = (g / (1.0 + jnp.exp(-g)) * u).astype(out_ref.dtype)


def hidden_of(c, mine, other, wg, wu, bg, bu, *after):
    t = mine.shape[1]
    q, d = wg.shape
    rank, _, m = bg.shape
    block = 304
    w_spec = pl.BlockSpec((block, d), lambda i: (i, 0))
    b_spec = pl.BlockSpec((rank, block, m), lambda i: (0, i, 0))
    t_spec = pl.BlockSpec(mine.shape, lambda i: (0, 0), pipeline_mode=pl.Buffered(1))
    return _call(
        _hidden_kernel,
        "hidden",
        flops=4 * q * t * (d + rank * m),
        moved=2 * (2 * q * d + d * t + 2 * rank * q * m + q * t),
        grid=(pl.cdiv(q, block),),
        in_specs=[SCALARS, t_spec, t_spec, w_spec, w_spec, b_spec, b_spec] + _any(len(after)),
        out_specs=pl.BlockSpec((block, t), lambda i: (i, 0)),
        out_shape=jax.ShapeDtypeStruct((q, t), bf16),
        scratch_shapes=[pltpu.VMEM((d, t), bf16), pltpu.VMEM((2 * rank * m, t), bf16)],
    )(c, mine, other, wg, wu, bg, bu, *after)


def local(tokens, w_gate, w_up, a_gate, a_up, b_gate, b_up, fitness):
    members, rank, d = a_gate.shape
    q = w_gate.shape[1]
    coeff = 1.0 / (members * lax.axis_size("z") * lax.axis_size("l") * rank) ** 0.5
    z, l, x, h, c = (lax.axis_index(a) for a in AXES)
    tok_t = tokens.T
    ag_t, au_t = (a.transpose(1, 2, 0) for a in (a_gate, a_up))
    bg, bu = (b.transpose(1, 2, 0) for b in (b_gate, b_up))
    block = (x - z - jnp.array(ORDER, jnp.int32)) % RING

    sg, su, rest = pack(tok_t, ag_t, au_t, fitness[None, :])
    bu_c = swap(bu, "c")

    def hop(axis, first, second):
        return swap(first, axis, 1), swap(second, axis, -1)

    one, three = hop("x", su, su)
    first = (2 * z + l) * 2 * d
    held = [lax.dynamic_slice_in_dim(w, first, 2 * d, 0) for w in (w_gate, w_up)]
    so = swap(rest, "h")
    one, three, bu_c, *held = join([one, three, bu_c, *held])
    at_y = (0, 2, 1, 3)
    sg_y = tie(sg, so)
    pa, pb = (
        lax.ppermute(sg_y, ("l", "h"), [(at_y[i], at_y[j]) for i, j in pairs])
        for pairs in (((1, 0), (2, 1), (0, 2)), ((3, 1), (1, 2), (2, 3)))
    )
    lo, hi, so = join([*hop("x", *halves(one, three)), so])
    su_x = (su, one, lo, hi, three)
    so = tie(so, lo)
    one, three = hop("x", so, so)
    ua = update(coeff, block, d, su_x, [bu, bu_c], so)
    gp_a, gm_a = hop("z", *ua[:2])
    one, three, pb = join([one, three, pb], ua[-1])
    lo, hi = hop("x", *halves(one, three))
    both = pick((2 * h + l).reshape(1), sg_y, pa, pb, rest, one)
    far_0 = swap(tie(bg, both), "l")
    lo, hi = join([lo, hi], both)
    so_x = (so, one, lo, hi, three)
    both = tie(both, lo)
    one, three = hop("x", both, both)
    gp_a, gm_a = join([gp_a, gm_a], both)
    ap, am = relay(gp_a, gm_a, *ua[2:4])
    fp_a, fm_a = hop("z", ap, am)
    ub = update(coeff, block, d, so_x, [bu, bu_c], ap)
    one, three = join([one, three], ap, ub[-1])
    lo, hi = hop("x", *halves(one, three))
    fp_a, fm_a = join([fp_a, fm_a], one)
    gp_b, gm_b = hop("z", *join(ub[:2], fp_a))
    lo, hi = join([lo, hi], fp_a)
    sg_x = (both, one, lo, hi, three)
    bg_c = swap(tie(bg, lo), "c")
    tok = tokens_of(jnp.stack([x, h]), sg_x, so_x, d, tok_t.shape[1], 2 * rank)
    tok_c = swap(tok, "c")
    gp_b, gm_b, far_0 = join([gp_b, gm_b, far_0], tok)
    ap, am = relay(gp_b, gm_b, *ub[2:4])
    fp_b, fm_b = hop("z", ap, am)
    fars = [v for far in (far_0,) for v in (far, swap(far, "c"))]
    gg = update(coeff, block, d, sg_x, [bg, bg_c, *fars], ap)
    fp_b, fm_b = join([fp_b, fm_b], gg[-1])
    gp_g, gm_g = hop("z", *gg[:2])
    keep, send = up_sums(
        (l == h).astype(jnp.int32).reshape(1), (ua[4], gp_a, gm_a, fp_a, fm_a), (ub[4], gp_b, gm_b, fp_b, fm_b)
    )
    sent = swap(send, "l")
    hidden = hidden_of(c.reshape(1), tok, tok_c, w_gate.T, w_up.T, bg, bu, gg[-1])
    gp_g, gm_g = join([gp_g, gm_g], hidden)
    ap, am = relay(gp_g, gm_g, *gg[2:4])
    fp_g, fm_g = hop("z", ap, am)
    at_c = c.reshape(1)
    gate_near, gate_far = gate_early(at_c, held[0], gg[4], gp_g, gm_g, ap)
    up_near, up_far = up_sum(keep, tie(sent, gate_near))
    new_up = renew(at_c, held[1], up_near, swap(up_far, "c"))
    fp_g, fm_g = join([fp_g, fm_g], gate_near)
    gate_near, gate_far = gate_late(gate_near, gate_far, fp_g, fm_g)
    new_gate = gate_rows(at_c, held[0], gate_near, swap(gate_far, "c"))
    return hidden.T, new_gate, new_up


def solution(mesh):
    fine = Mesh(mesh.devices.reshape(4, 2, 4, 2, 2), AXES)
    pop, mp = ("z", "l"), ("x", "h", "c")
    return jax.shard_map(
        local,
        mesh=fine,
        in_specs=(
            P(pop, mp),
            P(None, mp),
            P(None, mp),
            P(pop, None, mp),
            P(pop, None, mp),
            P(pop, None, mp),
            P(pop, None, mp),
            P(pop),
        ),
        out_specs=(P(pop, mp), P(pop, mp), P(pop, mp)),
        check_vma=False,
    )
```

```python
import functools

import jax
import jax.numpy as jnp
from jax import lax
from jax.experimental import pallas as pl
from jax.experimental.pallas import tpu as pltpu
from jax.sharding import Mesh
from jax.sharding import PartitionSpec as P

bf16 = jnp.bfloat16
f32 = jnp.float32
noise_scale = 0.5
AXES = ("z", "l", "x", "h", "c")
RING = 4
VMEM = 58 * 1024 * 1024
HINT = 1
NT = (((1,), (1,)), ((), ()))
TN = (((0,), (0,)), ((), ()))


def _call(kernel, name, flops=0, moved=0, **kw):
    return pl.pallas_call(
        kernel,
        name=name,
        compiler_params=pltpu.CompilerParams(vmem_limit_bytes=VMEM),
        cost_estimate=pl.CostEstimate(flops=flops // HINT, bytes_accessed=moved // HINT, transcendentals=0),
        **kw,
    )


def _any(n):
    return [pl.BlockSpec(memory_space=pl.ANY)] * n


FULL = pl.BlockSpec(memory_space=pltpu.VMEM)
SCALARS = pl.BlockSpec(memory_space=pltpu.SMEM)


def swap(v, axis, shift=1):
    n = lax.axis_size(axis)
    return lax.ppermute(v, axis, [(i, (i + shift) % n) for i in range(n)])


def join(vs, *after):
    n = len(vs)
    return _call(
        lambda *refs: None,
        "join",
        in_specs=_any(n + len(after)),
        out_specs=_any(n),
        out_shape=[jax.ShapeDtypeStruct(v.shape, v.dtype) for v in vs],
        input_output_aliases={i: i for i in range(n)},
    )(*vs, *after)


def tie(v, *after):
    return join([v], *after)[0]


def _own_mask(members, tokens):
    m = lax.broadcasted_iota(jnp.int32, (members, tokens), 0)
    t = lax.broadcasted_iota(jnp.int32, (members, tokens), 1)
    return jnp.logical_or(t == 2 * m, t == 2 * m + 1)


def _pack_kernel(tok_ref, ag_ref, au_ref, fit_ref, sg_ref, su_ref, all_ref):
    rank, d, m = ag_ref.shape
    tok = tok_ref[...]
    t = tok.shape[1]
    fit = fit_ref[...]
    mask = _own_mask(m, t)
    rows = []
    for a_ref, s_refs in ((ag_ref, (sg_ref,)), (au_ref, (su_ref, all_ref))):
        for r in range(rank):
            a = a_ref[r]
            for s_ref in s_refs:
                s_ref[r * d : (r + 1) * d, :] = (a.astype(f32) * fit).astype(bf16)
            s = lax.dot_general(a, tok, TN, preferred_element_type=f32)
            rows.append(jnp.sum(jnp.where(mask, s, 0.0), axis=0, keepdims=True))
    part = jnp.concatenate(rows, axis=0)
    high = part.astype(bf16)
    low = (part - high.astype(f32)).astype(bf16)
    at = rank * d
    for v in (tok, jnp.concatenate([high, low], axis=0)):
        for lo in range(0, t, m):
            all_ref[at : at + v.shape[0], :] = v[:, lo : lo + m]
            at += v.shape[0]


def pack(tok_t, ag, au, fit):
    rank, d, m = ag.shape
    t = tok_t.shape[1]
    pay = (d + 4 * rank) * (t // m)
    return _call(
        _pack_kernel,
        "pack",
        flops=4 * rank * d * m * t,
        moved=8 * rank * d * m,
        in_specs=[FULL] * 4,
        out_specs=[FULL] * 3,
        out_shape=[jax.ShapeDtypeStruct((n, m), bf16) for n in (rank * d, rank * d, rank * d + pay)],
    )(tok_t, ag, au, fit)


def _pick_kernel(y_ref, s_ref, pa_ref, pb_ref, all_ref, *refs):
    out_ref = refs[-1]
    n = s_ref.shape[0]
    y = y_ref[0]
    for where, at, ref in (
        (y == 1, 0, pb_ref),
        (y == 2, 0, pa_ref),
        (jnp.logical_or(y == 0, y == 3), 0, s_ref),
        (y < 2, n, pa_ref),
        (y >= 2, n, pb_ref),
    ):

        @pl.when(where)
        def _():
            out_ref[at : at + n, :] = ref[...]

    out_ref[2 * n :, :] = all_ref[n:, :]


def pick(y, s, pa, pb, rest, *after):
    n, m = s.shape
    return _call(
        _pick_kernel,
        "pick",
        moved=8 * s.size,
        in_specs=[SCALARS, FULL, FULL, FULL, FULL] + _any(len(after)),
        out_specs=FULL,
        out_shape=jax.ShapeDtypeStruct((n + rest.shape[0], m), s.dtype),
    )(y, s, pa, pb, rest, *after)


def rows_of(refs, lo, hi):
    if len(refs) == 1:
        return refs[0][lo:hi, :]
    n = refs[0].shape[0]
    parts = []
    if lo < n:
        parts.append(refs[0][lo : min(hi, n), :])
    if hi > n:
        parts.append(refs[1][max(lo, n) - n : hi - n, :])
    return parts[0] if len(parts) == 1 else jnp.concatenate(parts, axis=0)


def blocks_of(refs):
    own, one, two_lo, two_hi, three = refs
    return [own], [one], [two_lo, two_hi], [three]


PIECES = 5


ORDER = (2, 1, 3, 0)


def _update_kernel(coeff, slabs, d, rest, nb, nafter, block_ref, *refs):
    blocks = blocks_of(refs[:PIECES])
    b_refs = refs[PIECES : PIECES + nb]
    pp_ref, pm_ref, rp_ref, rm_ref, own_ref, lhs_ref, rhs_ref = refs[PIECES + nb + nafter :]
    m = b_refs[0].shape[2]
    n = d // 2
    i = pl.program_id(0)

    @pl.when(i == 0)
    def _():
        for step in range(RING):
            for j, block in enumerate(blocks):

                @pl.when(block_ref[step] == j)
                def _():
                    for k in range(slabs):
                        lhs_ref[step * d : (step + 1) * d, k * m : (k + 1) * m] = rows_of(block, k * d, (k + 1) * d)

    def put(acc):
        acc = (acc * coeff).astype(bf16)
        two, one, back, own = (acc[k * d : (k + 1) * d] for k in range(RING))
        w = acc.shape[1]
        pp_ref[:n, :w] = two[:n]
        pm_ref[:n, :w] = two[n:]
        pp_ref[n:, :w] = one[n:]
        rp_ref[:, :w] = one[:n]
        pm_ref[n:, :w] = back[:n]
        rm_ref[:, :w] = back[n:]
        own_ref[:, :w] = own

    slab = [(first, r) for first in range(0, nb, 2) for r in range(b_refs[first].shape[0])]
    for side in range(2):

        @pl.when(i == side)
        def _():
            for k, (first, r) in enumerate(slab):
                rhs_ref[:, k * m : (k + 1) * m] = b_refs[first + side][r]

    @pl.when(i < 2)
    def _():
        put(lax.dot_general(lhs_ref[...], rhs_ref[...], NT, preferred_element_type=f32))

    @pl.when(i == 2)
    def _():
        for k, (first, r) in enumerate(slab):
            for side in range(2):
                rhs_ref[side * rest : (side + 1) * rest, k * m : (k + 1) * m] = b_refs[first + side][r, :rest, :]
        put(lax.dot_general(lhs_ref[...], rhs_ref[: 2 * rest, :], NT, preferred_element_type=f32))


CUT = 1152


def update(coeff, block, rows, factors, seconds, *after):
    _, q, m = seconds[0].shape
    slabs = sum(b.shape[0] for b in seconds[::2])
    d = rows
    wide = 2 * q

    def once(shape):
        return pl.BlockSpec(shape, lambda i, w: (0,) * len(shape), pipeline_mode=pl.Buffered(1))

    def cut(n):
        return pl.BlockSpec((n, CUT), lambda i, w: (0, i))

    def near(b):
        return pl.BlockSpec((b.shape[0], CUT, m), lambda i, w: (0, jnp.minimum(i, 1), 0))

    def far(b):
        return pl.BlockSpec((b.shape[0], CUT, m), lambda i, w: (0, jnp.maximum(i - 1, 0), 0))

    sizes = (d, d, d // 2, d // 2, d)
    return _call(
        functools.partial(_update_kernel, coeff, slabs, d, q - CUT, len(seconds), len(after)),
        "update",
        flops=2 * RING * d * slabs * m * wide,
        moved=2 * (RING * slabs * d * m + slabs * m * wide + RING * d * wide),
        grid_spec=pltpu.PrefetchScalarGridSpec(
            num_scalar_prefetch=1,
            grid=(3,),
            in_specs=[once(f.shape) for f in factors] + [(near, far)[i % 2](b) for i, b in enumerate(seconds)] + _any(len(after)),
            out_specs=[cut(n) for n in sizes],
            scratch_shapes=[pltpu.VMEM((RING * d, slabs * m), bf16), pltpu.VMEM((CUT, slabs * m), bf16)],
        ),
        out_shape=[jax.ShapeDtypeStruct((n, wide), bf16) for n in sizes],
    )(block, *factors, *seconds, *after)


def _at(shape, row=0):
    return pl.BlockSpec(shape, lambda i: (row, 0))


def _relay_kernel(gp_ref, gm_ref, rp_ref, rm_ref, *refs):
    ap_ref, am_ref = refs[-2:]
    ap_ref[...] = (rp_ref[...].astype(f32) + gp_ref[...].astype(f32)).astype(bf16)
    am_ref[...] = (rm_ref[...].astype(f32) + gm_ref[...].astype(f32)).astype(bf16)


def relay(gp, gm, rp, rm, *after):
    spec = _at(rp.shape)
    return _call(
        _relay_kernel,
        "relay",
        grid=(1,),
        moved=12 * rp.size,
        in_specs=[spec] * 4 + _any(len(after)),
        out_specs=[spec] * 2,
        out_shape=[jax.ShapeDtypeStruct(rp.shape, bf16)] * 2,
    )(gp, gm, rp, rm, *after)


def _halves_kernel(one_ref, three_ref, *refs):
    lo_ref, hi_ref = refs[-2:]
    lo_ref[...] = one_ref[...]
    hi_ref[...] = three_ref[...]


def halves(one, three, *after):
    n, m = one.shape[0] // 2, one.shape[1]
    return _call(
        _halves_kernel,
        "halves",
        grid=(1,),
        moved=8 * n * m,
        in_specs=[_at((n, m)), _at((n, m), 1)] + _any(len(after)),
        out_specs=[_at((n, m))] * 2,
        out_shape=[jax.ShapeDtypeStruct((n, m), bf16)] * 2,
    )(one, three, *after)


def _total(own_ref, gp_ref, gm_ref, fp_ref, fm_ref):
    n = fp_ref.shape[0]
    first = own_ref[:n, :].astype(f32) + gm_ref[n:, :].astype(f32) + fp_ref[...].astype(f32)
    second = own_ref[n:, :].astype(f32) + gp_ref[n:, :].astype(f32) + fm_ref[...].astype(f32)
    return jnp.concatenate([first, second], axis=0)


def _split(total, near_ref, far_ref):
    q, k = near_ref.shape[1], CUT
    near_ref[:, :k] = total[:, :k]
    near_ref[:, k:] = total[:, 2 * k : k + q]
    far_ref[:, :k] = total[:, k : 2 * k].astype(far_ref.dtype)
    far_ref[:, k:] = total[:, k + q :].astype(far_ref.dtype)


def _ends(shape):
    d, q = shape[0], shape[1] // 2
    return [jax.ShapeDtypeStruct((d, q), f32), jax.ShapeDtypeStruct((d, q), bf16)]


def _gate_early_kernel(c_ref, held_ref, own_ref, gp_ref, gm_ref, *refs):
    near_ref, far_ref = refs[-2:]
    d = own_ref.shape[0]
    n = d // 2
    first = own_ref[:n, :].astype(f32) + gm_ref[n:, :].astype(f32)
    second = own_ref[n:, :].astype(f32) + gp_ref[n:, :].astype(f32)
    _split(jnp.concatenate([first, second], axis=0), near_ref, far_ref)
    near_ref[...] += held_ref[pl.ds(pl.multiple_of(c_ref[0] * d, d), d), :].astype(f32)


def gate_early(c, held, own, gp, gm, *after):
    d, q = own.shape[0], own.shape[1] // 2
    return _call(
        _gate_early_kernel,
        "gate_early",
        in_specs=[SCALARS] + [FULL] * 4 + _any(len(after)),
        out_specs=[FULL] * 2,
        out_shape=[jax.ShapeDtypeStruct((d, q), f32)] * 2,
    )(c, held, own, gp, gm, *after)


def _gate_late_kernel(near_ref, far_ref, fp_ref, fm_ref, out_ref, send_ref):
    n = fp_ref.shape[0]
    q, k = near_ref.shape[1], CUT
    for ref, rows in ((fp_ref, slice(0, n)), (fm_ref, slice(n, 2 * n))):
        out_ref[rows, :k] = (near_ref[rows, :k] + ref[:, :k].astype(f32)).astype(bf16)
        out_ref[rows, k:] = (near_ref[rows, k:] + ref[:, 2 * k : k + q].astype(f32)).astype(bf16)
        send_ref[rows, :k] = (far_ref[rows, :k] + ref[:, k : 2 * k].astype(f32)).astype(bf16)
        send_ref[rows, k:] = (far_ref[rows, k:] + ref[:, k + q :].astype(f32)).astype(bf16)


def gate_late(near, far, fp, fm):
    return _call(
        _gate_late_kernel,
        "gate_late",
        in_specs=[FULL] * 4,
        out_specs=[FULL] * 2,
        out_shape=[jax.ShapeDtypeStruct(near.shape, bf16)] * 2,
    )(near, far, fp, fm)


def _gate_rows_kernel(c_ref, held_ref, near_ref, far_ref, out_ref):
    d = near_ref.shape[0]
    c = c_ref[0]
    mine, other = pl.ds(pl.multiple_of(c * d, d), d), pl.ds(pl.multiple_of((1 - c) * d, d), d)
    out_ref[mine, :] = near_ref[...]
    out_ref[other, :] = (held_ref[other, :].astype(f32) + far_ref[...].astype(f32)).astype(bf16)


def gate_rows(c, held, near, far):
    return _call(
        _gate_rows_kernel,
        "gate_rows",
        in_specs=[SCALARS] + [FULL] * 3,
        out_specs=FULL,
        out_shape=jax.ShapeDtypeStruct(held.shape, bf16),
    )(c, held, near, far)


def _up_sums_kernel(mine_ref, *refs):
    keep_ref, send_ref = refs[10:]
    a, b = _total(*refs[:5]), _total(*refs[5:10])
    mine = mine_ref[0] == 1
    keep_ref[...] = jnp.where(mine, a, b)
    send_ref[...] = jnp.where(mine, b, a).astype(bf16)


def up_sums(mine, parts_a, parts_b, *after):
    shape = parts_a[0].shape

    def kernel(mine_ref, *refs):
        _up_sums_kernel(mine_ref, *refs[:10], *refs[-2:])

    return _call(
        kernel,
        "up_sums",
        in_specs=[SCALARS] + [FULL] * 10 + _any(len(after)),
        out_specs=[FULL] * 2,
        out_shape=[jax.ShapeDtypeStruct(shape, f32), jax.ShapeDtypeStruct(shape, bf16)],
    )(mine, *parts_a, *parts_b, *after)


def up_sum(keep, sent):
    def kernel(keep_ref, sent_ref, near_ref, far_ref):
        _split(keep_ref[...] + sent_ref[...].astype(f32), near_ref, far_ref)

    return _call(
        kernel,
        "up_sum",
        in_specs=[FULL] * 2,
        out_specs=[FULL] * 2,
        out_shape=_ends(keep.shape),
    )(keep, sent)


def _renew_kernel(c_ref, held_ref, near_ref, far_ref, out_ref):
    d = near_ref.shape[0]
    near, far = near_ref[...], far_ref[...].astype(f32)

    def put(first, second):
        out_ref[:d, :] = (held_ref[:d, :].astype(f32) + first).astype(bf16)
        out_ref[d:, :] = (held_ref[d:, :].astype(f32) + second).astype(bf16)

    @pl.when(c_ref[0] == 0)
    def _():
        put(near, far)

    @pl.when(c_ref[0] == 1)
    def _():
        put(far, near)


def renew(c, held, near, far):
    return _call(
        _renew_kernel,
        "renew",
        in_specs=[SCALARS] + [FULL] * 3,
        out_specs=FULL,
        out_shape=jax.ShapeDtypeStruct(held.shape, bf16),
    )(c, held, near, far)


def _tokens_kernel(n, at_ref, *refs):
    tok_ref = refs[-1]
    t, m = tok_ref.shape[1], refs[0].shape[1]
    d = (tok_ref.shape[0] - 2 * n) // (2 * RING)
    x, h = at_ref[0], at_ref[1]
    wide = t // m
    total = None
    for s in range(2):
        gather = refs[s * PIECES : (s + 1) * PIECES]
        start = gather[0].shape[0] - wide * (d + 2 * n)
        for j, block in enumerate(blocks_of(gather)):
            rows = [rows_of(block, start + i * d, start + (i + 1) * d) for i in range(wide)]
            to = 2 * lax.rem(x + RING - j, RING) + (h if s == 0 else 1 - h)
            tok_ref[pl.ds(pl.multiple_of(to * d, d), d), :] = jnp.concatenate(rows, axis=1)
            at = start + wide * d
            terms = [rows_of(block, at + i * 2 * n, at + (i + 1) * 2 * n).astype(f32) for i in range(wide)]
            both = jnp.concatenate(terms, axis=1)
            value = both[:n] + both[n:]
            total = value if total is None else total + value
    high = total.astype(bf16)
    low = (total - high.astype(f32)).astype(bf16)
    tok_ref[2 * RING * d :, :] = jnp.concatenate([high, low], axis=0)


def tokens_of(at, own, other, d, t, probes, *after):
    return _call(
        functools.partial(_tokens_kernel, probes),
        "tokens",
        moved=8 * RING * 2 * d * t,
        in_specs=[SCALARS] + [FULL] * (2 * PIECES) + _any(len(after)),
        out_specs=FULL,
        out_shape=jax.ShapeDtypeStruct((2 * RING * d + 2 * probes, t), bf16),
    )(at, *own, *other, *after)


def _hidden_kernel(c_ref, mine_ref, other_ref, wg_ref, wu_ref, bg_ref, bu_ref, *refs):
    out_ref, tok_ref, p_ref = refs[-3:]
    rank, _, m = bg_ref.shape
    t = mine_ref.shape[1]
    n = 2 * rank
    d = (mine_ref.shape[0] - 2 * n) // (2 * RING)

    @pl.when(pl.program_id(0) == 0)
    def _():
        c = c_ref[0]
        for ref, core in ((mine_ref, c), (other_ref, 1 - c)):
            for i in range(2 * RING):
                tok_ref[pl.ds(pl.multiple_of((2 * i + core) * d, d), d), :] = ref[i * d : (i + 1) * d, :]
        mask = _own_mask(m, t)
        terms = mine_ref[2 * RING * d :, :].astype(f32) + other_ref[2 * RING * d :, :].astype(f32)
        probe = (terms[:n] + terms[n:]).astype(bf16).astype(f32) * noise_scale
        for i in range(2 * rank):
            row = jnp.broadcast_to(probe[i : i + 1, :], (m, t))
            p_ref[i * m : (i + 1) * m, :] = jnp.where(mask, row, 0.0).astype(bf16)

    pre = []
    for k, (w_ref, b_ref) in enumerate(((wg_ref, bg_ref), (wu_ref, bu_ref))):
        b = jnp.concatenate([b_ref[r] for r in range(rank)], axis=1)
        acc = jnp.dot(w_ref[...], tok_ref[...], preferred_element_type=f32)
        acc += jnp.dot(b, p_ref[k * rank * m : (k + 1) * rank * m, :], preferred_element_type=f32)
        pre.append(acc)
    g, u = pre
    out_ref[...] = (g / (1.0 + jnp.exp(-g)) * u).astype(out_ref.dtype)


def hidden_of(c, mine, other, wg, wu, bg, bu, *after):
    t = mine.shape[1]
    q, d = wg.shape
    rank, _, m = bg.shape
    block = 304
    w_spec = pl.BlockSpec((block, d), lambda i: (i, 0))
    b_spec = pl.BlockSpec((rank, block, m), lambda i: (0, i, 0))
    t_spec = pl.BlockSpec(mine.shape, lambda i: (0, 0), pipeline_mode=pl.Buffered(1))
    return _call(
        _hidden_kernel,
        "hidden",
        flops=4 * q * t * (d + rank * m),
        moved=2 * (2 * q * d + d * t + 2 * rank * q * m + q * t),
        grid=(pl.cdiv(q, block),),
        in_specs=[SCALARS, t_spec, t_spec, w_spec, w_spec, b_spec, b_spec] + _any(len(after)),
        out_specs=pl.BlockSpec((block, t), lambda i: (i, 0)),
        out_shape=jax.ShapeDtypeStruct((q, t), bf16),
        scratch_shapes=[pltpu.VMEM((d, t), bf16), pltpu.VMEM((2 * rank * m, t), bf16)],
    )(c, mine, other, wg, wu, bg, bu, *after)


def local(tokens, w_gate, w_up, a_gate, a_up, b_gate, b_up, fitness):
    members, rank, d = a_gate.shape
    q = w_gate.shape[1]
    coeff = 1.0 / (members * lax.axis_size("z") * lax.axis_size("l") * rank) ** 0.5
    z, l, x, h, c = (lax.axis_index(a) for a in AXES)
    tok_t = tokens.T
    ag_t, au_t = (a.transpose(1, 2, 0) for a in (a_gate, a_up))
    bg, bu = (b.transpose(1, 2, 0) for b in (b_gate, b_up))
    block = (x - z - jnp.array(ORDER, jnp.int32)) % RING

    sg, su, rest = pack(tok_t, ag_t, au_t, fitness[None, :])
    bu_c = swap(bu, "c")

    def hop(axis, first, second):
        return swap(first, axis, 1), swap(second, axis, -1)

    one, three = hop("x", su, su)
    first = (2 * z + l) * 2 * d
    held = [lax.dynamic_slice_in_dim(w, first, 2 * d, 0) for w in (w_gate, w_up)]
    so = swap(rest, "h")
    one, three, bu_c, *held = join([one, three, bu_c, *held])
    at_y = (0, 2, 1, 3)
    sg_y = tie(sg, so)
    pa, pb = (
        lax.ppermute(sg_y, ("l", "h"), [(at_y[i], at_y[j]) for i, j in pairs])
        for pairs in (((1, 0), (2, 1), (0, 2)), ((3, 1), (1, 2), (2, 3)))
    )
    lo, hi, so = join([*hop("x", *halves(one, three)), so])
    su_x = (su, one, lo, hi, three)
    so = tie(so, lo)
    one, three = hop("x", so, so)
    ua = update(coeff, block, d, su_x, [bu, bu_c], so)
    gp_a, gm_a = hop("z", *ua[:2])
    one, three, pb = join([one, three, pb], ua[-1])
    lo, hi = hop("x", *halves(one, three))
    both = pick((2 * h + l).reshape(1), sg_y, pa, pb, rest, one)
    far_0 = swap(tie(bg, both), "l")
    lo, hi = join([lo, hi], both)
    so_x = (so, one, lo, hi, three)
    both = tie(both, lo)
    one, three = hop("x", both, both)
    gp_a, gm_a = join([gp_a, gm_a], both)
    ap, am = relay(gp_a, gm_a, *ua[2:4])
    fp_a, fm_a = hop("z", ap, am)
    ub = update(coeff, block, d, so_x, [bu, bu_c], ap)
    one, three = join([one, three], ap, ub[-1])
    lo, hi = hop("x", *halves(one, three))
    fp_a, fm_a = join([fp_a, fm_a], one)
    gp_b, gm_b = hop("z", *join(ub[:2], fp_a))
    lo, hi = join([lo, hi], fp_a)
    sg_x = (both, one, lo, hi, three)
    bg_c = swap(tie(bg, lo), "c")
    tok = tokens_of(jnp.stack([x, h]), sg_x, so_x, d, tok_t.shape[1], 2 * rank)
    tok_c = swap(tok, "c")
    gp_b, gm_b, far_0 = join([gp_b, gm_b, far_0], tok)
    ap, am = relay(gp_b, gm_b, *ub[2:4])
    fp_b, fm_b = hop("z", ap, am)
    fars = [v for far in (far_0,) for v in (far, swap(far, "c"))]
    gg = update(coeff, block, d, sg_x, [bg, bg_c, *fars], ap)
    fp_b, fm_b = join([fp_b, fm_b], gg[-1])
    gp_g, gm_g = hop("z", *gg[:2])
    keep, send = up_sums(
        (l == h).astype(jnp.int32).reshape(1), (ua[4], gp_a, gm_a, fp_a, fm_a), (ub[4], gp_b, gm_b, fp_b, fm_b)
    )
    sent = swap(send, "l")
    hidden = hidden_of(c.reshape(1), tok, tok_c, w_gate.T, w_up.T, bg, bu, gg[-1])
    gp_g, gm_g = join([gp_g, gm_g], hidden)
    ap, am = relay(gp_g, gm_g, *gg[2:4])
    fp_g, fm_g = hop("z", ap, am)
    at_c = c.reshape(1)
    gate_near, gate_far = gate_early(at_c, held[0], gg[4], gp_g, gm_g, ap)
    up_near, up_far = up_sum(keep, tie(sent, gate_near))
    new_up = renew(at_c, held[1], up_near, swap(up_far, "c"))
    fp_g, fm_g = join([fp_g, fm_g], gate_near)
    gate_near, gate_far = gate_late(gate_near, gate_far, fp_g, fm_g)
    new_gate = gate_rows(at_c, held[0], gate_near, swap(gate_far, "c"))
    return hidden.T, new_gate, new_up


def solution(mesh):
    fine = Mesh(mesh.devices.reshape(4, 2, 4, 2, 2), AXES)
    pop, mp = ("z", "l"), ("x", "h", "c")
    return jax.shard_map(
        local,
        mesh=fine,
        in_specs=(
            P(pop, mp),
            P(None, mp),
            P(None, mp),
            P(pop, None, mp),
            P(pop, None, mp),
            P(pop, None, mp),
            P(pop, None, mp),
            P(pop),
        ),
        out_specs=(P(pop, mp), P(pop, mp), P(pop, mp)),
        check_vma=False,
    )
```

```python
import functools

import jax
import jax.numpy as jnp
from jax import lax
from jax.experimental import pallas as pl
from jax.experimental.pallas import tpu as pltpu
from jax.sharding import Mesh
from jax.sharding import PartitionSpec as P

bf16 = jnp.bfloat16
f32 = jnp.float32
noise_scale = 0.5
AXES = ("z", "l", "x", "h", "c")
RING = 4
VMEM = 58 * 1024 * 1024
HINT = 1
NT = (((1,), (1,)), ((), ()))
TN = (((0,), (0,)), ((), ()))


def _call(kernel, name, flops=0, moved=0, **kw):
    return pl.pallas_call(
        kernel,
        name=name,
        compiler_params=pltpu.CompilerParams(vmem_limit_bytes=VMEM),
        cost_estimate=pl.CostEstimate(flops=flops // HINT, bytes_accessed=moved // HINT, transcendentals=0),
        **kw,
    )


def _any(n):
    return [pl.BlockSpec(memory_space=pl.ANY)] * n


FULL = pl.BlockSpec(memory_space=pltpu.VMEM)
SCALARS = pl.BlockSpec(memory_space=pltpu.SMEM)


def swap(v, axis, shift=1):
    n = lax.axis_size(axis)
    return lax.ppermute(v, axis, [(i, (i + shift) % n) for i in range(n)])


def join(vs, *after):
    n = len(vs)
    return _call(
        lambda *refs: None,
        "join",
        in_specs=_any(n + len(after)),
        out_specs=_any(n),
        out_shape=[jax.ShapeDtypeStruct(v.shape, v.dtype) for v in vs],
        input_output_aliases={i: i for i in range(n)},
    )(*vs, *after)


def tie(v, *after):
    return join([v], *after)[0]


def _own_mask(members, tokens):
    m = lax.broadcasted_iota(jnp.int32, (members, tokens), 0)
    t = lax.broadcasted_iota(jnp.int32, (members, tokens), 1)
    return jnp.logical_or(t == 2 * m, t == 2 * m + 1)


def _pack_kernel(tok_ref, ag_ref, au_ref, fit_ref, sg_ref, su_ref, all_ref):
    rank, d, m = ag_ref.shape
    tok = tok_ref[...]
    t = tok.shape[1]
    fit = fit_ref[...]
    mask = _own_mask(m, t)
    rows = []
    for a_ref, s_refs in ((ag_ref, (sg_ref,)), (au_ref, (su_ref, all_ref))):
        for r in range(rank):
            a = a_ref[r]
            for s_ref in s_refs:
                s_ref[r * d : (r + 1) * d, :] = (a.astype(f32) * fit).astype(bf16)
            s = lax.dot_general(a, tok, TN, preferred_element_type=f32)
            rows.append(jnp.sum(jnp.where(mask, s, 0.0), axis=0, keepdims=True))
    part = jnp.concatenate(rows, axis=0)
    high = part.astype(bf16)
    low = (part - high.astype(f32)).astype(bf16)
    at = rank * d
    for v in (tok, jnp.concatenate([high, low], axis=0)):
        for lo in range(0, t, m):
            all_ref[at : at + v.shape[0], :] = v[:, lo : lo + m]
            at += v.shape[0]


def pack(tok_t, ag, au, fit):
    rank, d, m = ag.shape
    t = tok_t.shape[1]
    pay = (d + 4 * rank) * (t // m)
    return _call(
        _pack_kernel,
        "pack",
        flops=4 * rank * d * m * t,
        moved=8 * rank * d * m,
        in_specs=[FULL] * 4,
        out_specs=[FULL] * 3,
        out_shape=[jax.ShapeDtypeStruct((n, m), bf16) for n in (rank * d, rank * d, rank * d + pay)],
    )(tok_t, ag, au, fit)


def _pick_kernel(y_ref, s_ref, pa_ref, pb_ref, all_ref, *refs):
    out_ref = refs[-1]
    n = s_ref.shape[0]
    y = y_ref[0]
    for where, at, ref in (
        (y == 1, 0, pb_ref),
        (y == 2, 0, pa_ref),
        (jnp.logical_or(y == 0, y == 3), 0, s_ref),
        (y < 2, n, pa_ref),
        (y >= 2, n, pb_ref),
    ):

        @pl.when(where)
        def _():
            out_ref[at : at + n, :] = ref[...]

    out_ref[2 * n :, :] = all_ref[n:, :]


def pick(y, s, pa, pb, rest, *after):
    n, m = s.shape
    return _call(
        _pick_kernel,
        "pick",
        moved=8 * s.size,
        in_specs=[SCALARS, FULL, FULL, FULL, FULL] + _any(len(after)),
        out_specs=FULL,
        out_shape=jax.ShapeDtypeStruct((n + rest.shape[0], m), s.dtype),
    )(y, s, pa, pb, rest, *after)


def rows_of(refs, lo, hi):
    if len(refs) == 1:
        return refs[0][lo:hi, :]
    n = refs[0].shape[0]
    parts = []
    if lo < n:
        parts.append(refs[0][lo : min(hi, n), :])
    if hi > n:
        parts.append(refs[1][max(lo, n) - n : hi - n, :])
    return parts[0] if len(parts) == 1 else jnp.concatenate(parts, axis=0)


def blocks_of(refs):
    own, one, two_lo, two_hi, three = refs
    return [own], [one], [two_lo, two_hi], [three]


PIECES = 5


ORDER = (2, 1, 3, 0)


def _update_kernel(coeff, slabs, d, rest, nb, nafter, block_ref, *refs):
    blocks = blocks_of(refs[:PIECES])
    b_refs = refs[PIECES : PIECES + nb]
    pp_ref, pm_ref, rp_ref, rm_ref, own_ref, lhs_ref, rhs_ref = refs[PIECES + nb + nafter :]
    m = b_refs[0].shape[2]
    n = d // 2
    i = pl.program_id(0)

    @pl.when(i == 0)
    def _():
        for step in range(RING):
            for j, block in enumerate(blocks):

                @pl.when(block_ref[step] == j)
                def _():
                    for k in range(slabs):
                        lhs_ref[step * d : (step + 1) * d, k * m : (k + 1) * m] = rows_of(block, k * d, (k + 1) * d)

    def put(acc):
        acc = (acc * coeff).astype(bf16)
        two, one, back, own = (acc[k * d : (k + 1) * d] for k in range(RING))
        w = acc.shape[1]
        pp_ref[:n, :w] = two[:n]
        pm_ref[:n, :w] = two[n:]
        pp_ref[n:, :w] = one[n:]
        rp_ref[:, :w] = one[:n]
        pm_ref[n:, :w] = back[:n]
        rm_ref[:, :w] = back[n:]
        own_ref[:, :w] = own

    slab = [(first, r) for first in range(0, nb, 2) for r in range(b_refs[first].shape[0])]
    for side in range(2):

        @pl.when(i == side)
        def _():
            for k, (first, r) in enumerate(slab):
                rhs_ref[:, k * m : (k + 1) * m] = b_refs[first + side][r]

    @pl.when(i < 2)
    def _():
        put(lax.dot_general(lhs_ref[...], rhs_ref[...], NT, preferred_element_type=f32))

    @pl.when(i == 2)
    def _():
        for k, (first, r) in enumerate(slab):
            for side in range(2):
                rhs_ref[side * rest : (side + 1) * rest, k * m : (k + 1) * m] = b_refs[first + side][r, :rest, :]
        put(lax.dot_general(lhs_ref[...], rhs_ref[: 2 * rest, :], NT, preferred_element_type=f32))


CUT = 1152


def update(coeff, block, rows, factors, seconds, *after):
    _, q, m = seconds[0].shape
    slabs = sum(b.shape[0] for b in seconds[::2])
    d = rows
    wide = 2 * q

    def once(shape):
        return pl.BlockSpec(shape, lambda i, w: (0,) * len(shape), pipeline_mode=pl.Buffered(1))

    def cut(n):
        return pl.BlockSpec((n, CUT), lambda i, w: (0, i))

    def near(b):
        return pl.BlockSpec((b.shape[0], CUT, m), lambda i, w: (0, jnp.minimum(i, 1), 0))

    def far(b):
        return pl.BlockSpec((b.shape[0], CUT, m), lambda i, w: (0, jnp.maximum(i - 1, 0), 0))

    sizes = (d, d, d // 2, d // 2, d)
    return _call(
        functools.partial(_update_kernel, coeff, slabs, d, q - CUT, len(seconds), len(after)),
        "update",
        flops=2 * RING * d * slabs * m * wide,
        moved=2 * (RING * slabs * d * m + slabs * m * wide + RING * d * wide),
        grid_spec=pltpu.PrefetchScalarGridSpec(
            num_scalar_prefetch=1,
            grid=(3,),
            in_specs=[once(f.shape) for f in factors] + [(near, far)[i % 2](b) for i, b in enumerate(seconds)] + _any(len(after)),
            out_specs=[cut(n) for n in sizes],
            scratch_shapes=[pltpu.VMEM((RING * d, slabs * m), bf16), pltpu.VMEM((CUT, slabs * m), bf16)],
        ),
        out_shape=[jax.ShapeDtypeStruct((n, wide), bf16) for n in sizes],
    )(block, *factors, *seconds, *after)


def _at(shape, row=0):
    return pl.BlockSpec(shape, lambda i: (row, 0))


WIDE = 1280


def _relay_kernel(gp_ref, gm_ref, rp_ref, rm_ref, *refs):
    ap_ref, am_ref = refs[-2:]
    ap_ref[...] = (rp_ref[...].astype(f32) + gp_ref[...].astype(f32)).astype(bf16)
    am_ref[...] = (rm_ref[...].astype(f32) + gm_ref[...].astype(f32)).astype(bf16)


def relay(gp, gm, rp, rm, *after):
    spec = pl.BlockSpec((rp.shape[0], WIDE), lambda i: (0, i))
    return _call(
        _relay_kernel,
        "relay",
        grid=(2,),
        moved=12 * rp.size,
        in_specs=[spec] * 4 + _any(len(after)),
        out_specs=[spec] * 2,
        out_shape=[jax.ShapeDtypeStruct(rp.shape, bf16)] * 2,
    )(gp, gm, rp, rm, *after)


def _halves_kernel(one_ref, three_ref, *refs):
    lo_ref, hi_ref = refs[-2:]
    lo_ref[...] = one_ref[...]
    hi_ref[...] = three_ref[...]


def halves(one, three, *after):
    n, m = one.shape[0] // 2, one.shape[1]
    return _call(
        _halves_kernel,
        "halves",
        grid=(1,),
        moved=8 * n * m,
        in_specs=[_at((n, m)), _at((n, m), 1)] + _any(len(after)),
        out_specs=[_at((n, m))] * 2,
        out_shape=[jax.ShapeDtypeStruct((n, m), bf16)] * 2,
    )(one, three, *after)


def _total(own_ref, gp_ref, gm_ref, fp_ref, fm_ref):
    n = fp_ref.shape[0]
    first = own_ref[:n, :].astype(f32) + gm_ref[n:, :].astype(f32) + fp_ref[...].astype(f32)
    second = own_ref[n:, :].astype(f32) + gp_ref[n:, :].astype(f32) + fm_ref[...].astype(f32)
    return jnp.concatenate([first, second], axis=0)


def _split(total, near_ref, far_ref):
    q, k = near_ref.shape[1], CUT
    near_ref[:, :k] = total[:, :k]
    near_ref[:, k:] = total[:, 2 * k : k + q]
    far_ref[:, :k] = total[:, k : 2 * k].astype(far_ref.dtype)
    far_ref[:, k:] = total[:, k + q :].astype(far_ref.dtype)


def _ends(shape):
    d, q = shape[0], shape[1] // 2
    return [jax.ShapeDtypeStruct((d, q), f32), jax.ShapeDtypeStruct((d, q), bf16)]


def _gate_early_kernel(c_ref, held_ref, own_ref, gp_ref, gm_ref, *refs):
    near_ref, far_ref = refs[-2:]
    d = own_ref.shape[0]
    n = d // 2
    first = own_ref[:n, :].astype(f32) + gm_ref[n:, :].astype(f32)
    second = own_ref[n:, :].astype(f32) + gp_ref[n:, :].astype(f32)
    _split(jnp.concatenate([first, second], axis=0), near_ref, far_ref)
    near_ref[...] += held_ref[pl.ds(pl.multiple_of(c_ref[0] * d, d), d), :].astype(f32)


def gate_early(c, held, own, gp, gm, *after):
    d, q = own.shape[0], own.shape[1] // 2
    return _call(
        _gate_early_kernel,
        "gate_early",
        in_specs=[SCALARS] + [FULL] * 4 + _any(len(after)),
        out_specs=[FULL] * 2,
        out_shape=[jax.ShapeDtypeStruct((d, q), f32)] * 2,
    )(c, held, own, gp, gm, *after)


def _gate_late_kernel(near_ref, far_ref, fp_ref, fm_ref, out_ref, send_ref):
    n = fp_ref.shape[0]
    q, k = near_ref.shape[1], CUT
    for ref, rows in ((fp_ref, slice(0, n)), (fm_ref, slice(n, 2 * n))):
        out_ref[rows, :k] = (near_ref[rows, :k] + ref[:, :k].astype(f32)).astype(bf16)
        out_ref[rows, k:] = (near_ref[rows, k:] + ref[:, 2 * k : k + q].astype(f32)).astype(bf16)
        send_ref[rows, :k] = (far_ref[rows, :k] + ref[:, k : 2 * k].astype(f32)).astype(bf16)
        send_ref[rows, k:] = (far_ref[rows, k:] + ref[:, k + q :].astype(f32)).astype(bf16)


def gate_late(near, far, fp, fm):
    return _call(
        _gate_late_kernel,
        "gate_late",
        in_specs=[FULL] * 4,
        out_specs=[FULL] * 2,
        out_shape=[jax.ShapeDtypeStruct(near.shape, bf16)] * 2,
    )(near, far, fp, fm)


def _gate_rows_kernel(c_ref, held_ref, near_ref, far_ref, out_ref):
    d = near_ref.shape[0]
    c = c_ref[0]
    mine, other = pl.ds(pl.multiple_of(c * d, d), d), pl.ds(pl.multiple_of((1 - c) * d, d), d)
    out_ref[mine, :] = near_ref[...]
    out_ref[other, :] = (held_ref[other, :].astype(f32) + far_ref[...].astype(f32)).astype(bf16)


def gate_rows(c, held, near, far):
    return _call(
        _gate_rows_kernel,
        "gate_rows",
        in_specs=[SCALARS] + [FULL] * 3,
        out_specs=FULL,
        out_shape=jax.ShapeDtypeStruct(held.shape, bf16),
    )(c, held, near, far)


def _up_sums_kernel(mine_ref, *refs):
    keep_ref, send_ref = refs[10:]
    a, b = _total(*refs[:5]), _total(*refs[5:10])
    mine = mine_ref[0] == 1
    keep_ref[...] = jnp.where(mine, a, b)
    send_ref[...] = jnp.where(mine, b, a).astype(bf16)


def up_sums(mine, parts_a, parts_b, *after):
    shape = parts_a[0].shape

    def kernel(mine_ref, *refs):
        _up_sums_kernel(mine_ref, *refs[:10], *refs[-2:])

    return _call(
        kernel,
        "up_sums",
        grid=(2,),
        in_specs=[SCALARS] + [pl.BlockSpec((p.shape[0], WIDE), lambda i: (0, i)) for p in (*parts_a, *parts_b)] + _any(len(after)),
        out_specs=[pl.BlockSpec((shape[0], WIDE), lambda i: (0, i))] * 2,
        out_shape=[jax.ShapeDtypeStruct(shape, f32), jax.ShapeDtypeStruct(shape, bf16)],
    )(mine, *parts_a, *parts_b, *after)


def up_sum(keep, sent):
    def kernel(keep_ref, sent_ref, near_ref, far_ref):
        _split(keep_ref[...] + sent_ref[...].astype(f32), near_ref, far_ref)

    return _call(
        kernel,
        "up_sum",
        in_specs=[FULL] * 2,
        out_specs=[FULL] * 2,
        out_shape=_ends(keep.shape),
    )(keep, sent)


def _renew_kernel(c_ref, held_ref, near_ref, far_ref, out_ref):
    d = near_ref.shape[0]
    near, far = near_ref[...], far_ref[...].astype(f32)

    def put(first, second):
        out_ref[:d, :] = (held_ref[:d, :].astype(f32) + first).astype(bf16)
        out_ref[d:, :] = (held_ref[d:, :].astype(f32) + second).astype(bf16)

    @pl.when(c_ref[0] == 0)
    def _():
        put(near, far)

    @pl.when(c_ref[0] == 1)
    def _():
        put(far, near)


def renew(c, held, near, far):
    return _call(
        _renew_kernel,
        "renew",
        in_specs=[SCALARS] + [FULL] * 3,
        out_specs=FULL,
        out_shape=jax.ShapeDtypeStruct(held.shape, bf16),
    )(c, held, near, far)


def _tokens_kernel(n, at_ref, *refs):
    tok_ref = refs[-1]
    t, m = tok_ref.shape[1], refs[0].shape[1]
    d = (tok_ref.shape[0] - 2 * n) // (2 * RING)
    x, h = at_ref[0], at_ref[1]
    wide = t // m
    total = None
    for s in range(2):
        gather = refs[s * PIECES : (s + 1) * PIECES]
        start = gather[0].shape[0] - wide * (d + 2 * n)
        for j, block in enumerate(blocks_of(gather)):
            rows = [rows_of(block, start + i * d, start + (i + 1) * d) for i in range(wide)]
            to = 2 * lax.rem(x + RING - j, RING) + (h if s == 0 else 1 - h)
            tok_ref[pl.ds(pl.multiple_of(to * d, d), d), :] = jnp.concatenate(rows, axis=1)
            at = start + wide * d
            terms = [rows_of(block, at + i * 2 * n, at + (i + 1) * 2 * n).astype(f32) for i in range(wide)]
            both = jnp.concatenate(terms, axis=1)
            value = both[:n] + both[n:]
            total = value if total is None else total + value
    high = total.astype(bf16)
    low = (total - high.astype(f32)).astype(bf16)
    tok_ref[2 * RING * d :, :] = jnp.concatenate([high, low], axis=0)


def tokens_of(at, own, other, d, t, probes, *after):
    return _call(
        functools.partial(_tokens_kernel, probes),
        "tokens",
        moved=8 * RING * 2 * d * t,
        in_specs=[SCALARS] + [FULL] * (2 * PIECES) + _any(len(after)),
        out_specs=FULL,
        out_shape=jax.ShapeDtypeStruct((2 * RING * d + 2 * probes, t), bf16),
    )(at, *own, *other, *after)


def _hidden_kernel(c_ref, mine_ref, other_ref, wg_ref, wu_ref, bg_ref, bu_ref, *refs):
    out_ref, tok_ref, p_ref = refs[-3:]
    rank, _, m = bg_ref.shape
    t = mine_ref.shape[1]
    n = 2 * rank
    d = (mine_ref.shape[0] - 2 * n) // (2 * RING)

    @pl.when(pl.program_id(0) == 0)
    def _():
        c = c_ref[0]
        for ref, core in ((mine_ref, c), (other_ref, 1 - c)):
            for i in range(2 * RING):
                tok_ref[pl.ds(pl.multiple_of((2 * i + core) * d, d), d), :] = ref[i * d : (i + 1) * d, :]
        mask = _own_mask(m, t)
        terms = mine_ref[2 * RING * d :, :].astype(f32) + other_ref[2 * RING * d :, :].astype(f32)
        probe = (terms[:n] + terms[n:]).astype(bf16).astype(f32) * noise_scale
        for i in range(2 * rank):
            row = jnp.broadcast_to(probe[i : i + 1, :], (m, t))
            p_ref[i * m : (i + 1) * m, :] = jnp.where(mask, row, 0.0).astype(bf16)

    pre = []
    for k, (w_ref, b_ref) in enumerate(((wg_ref, bg_ref), (wu_ref, bu_ref))):
        b = jnp.concatenate([b_ref[r] for r in range(rank)], axis=1)
        acc = jnp.dot(w_ref[...], tok_ref[...], preferred_element_type=f32)
        acc += jnp.dot(b, p_ref[k * rank * m : (k + 1) * rank * m, :], preferred_element_type=f32)
        pre.append(acc)
    g, u = pre
    out_ref[...] = (g / (1.0 + jnp.exp(-g)) * u).astype(out_ref.dtype)


def hidden_of(c, mine, other, wg, wu, bg, bu, *after):
    t = mine.shape[1]
    q, d = wg.shape
    rank, _, m = bg.shape
    block = 304
    w_spec = pl.BlockSpec((block, d), lambda i: (i, 0))
    b_spec = pl.BlockSpec((rank, block, m), lambda i: (0, i, 0))
    t_spec = pl.BlockSpec(mine.shape, lambda i: (0, 0), pipeline_mode=pl.Buffered(1))
    return _call(
        _hidden_kernel,
        "hidden",
        flops=4 * q * t * (d + rank * m),
        moved=2 * (2 * q * d + d * t + 2 * rank * q * m + q * t),
        grid=(pl.cdiv(q, block),),
        in_specs=[SCALARS, t_spec, t_spec, w_spec, w_spec, b_spec, b_spec] + _any(len(after)),
        out_specs=pl.BlockSpec((block, t), lambda i: (i, 0)),
        out_shape=jax.ShapeDtypeStruct((q, t), bf16),
        scratch_shapes=[pltpu.VMEM((d, t), bf16), pltpu.VMEM((2 * rank * m, t), bf16)],
    )(c, mine, other, wg, wu, bg, bu, *after)


def local(tokens, w_gate, w_up, a_gate, a_up, b_gate, b_up, fitness):
    members, rank, d = a_gate.shape
    q = w_gate.shape[1]
    coeff = 1.0 / (members * lax.axis_size("z") * lax.axis_size("l") * rank) ** 0.5
    z, l, x, h, c = (lax.axis_index(a) for a in AXES)
    tok_t = tokens.T
    ag_t, au_t = (a.transpose(1, 2, 0) for a in (a_gate, a_up))
    bg, bu = (b.transpose(1, 2, 0) for b in (b_gate, b_up))
    block = (x - z - jnp.array(ORDER, jnp.int32)) % RING

    sg, su, rest = pack(tok_t, ag_t, au_t, fitness[None, :])
    bu_c = swap(bu, "c")

    def hop(axis, first, second):
        return swap(first, axis, 1), swap(second, axis, -1)

    one, three = hop("x", su, su)
    first = (2 * z + l) * 2 * d
    held = [lax.dynamic_slice_in_dim(w, first, 2 * d, 0) for w in (w_gate, w_up)]
    so = swap(rest, "h")
    one, three, bu_c, *held = join([one, three, bu_c, *held])
    at_y = (0, 2, 1, 3)
    sg_y = tie(sg, so)
    pa, pb = (
        lax.ppermute(sg_y, ("l", "h"), [(at_y[i], at_y[j]) for i, j in pairs])
        for pairs in (((1, 0), (2, 1), (0, 2)), ((3, 1), (1, 2), (2, 3)))
    )
    lo, hi, so = join([*hop("x", *halves(one, three)), so])
    su_x = (su, one, lo, hi, three)
    so = tie(so, lo)
    one, three = hop("x", so, so)
    ua = update(coeff, block, d, su_x, [bu, bu_c], so)
    gp_a, gm_a = hop("z", *ua[:2])
    one, three, pb = join([one, three, pb], ua[-1])
    lo, hi = hop("x", *halves(one, three))
    both = pick((2 * h + l).reshape(1), sg_y, pa, pb, rest, one)
    far_0 = swap(tie(bg, both), "l")
    lo, hi = join([lo, hi], both)
    so_x = (so, one, lo, hi, three)
    both = tie(both, lo)
    one, three = hop("x", both, both)
    gp_a, gm_a = join([gp_a, gm_a], both)
    ap, am = relay(gp_a, gm_a, *ua[2:4])
    fp_a, fm_a = hop("z", ap, am)
    ub = update(coeff, block, d, so_x, [bu, bu_c], ap)
    one, three = join([one, three], ap, ub[-1])
    lo, hi = hop("x", *halves(one, three))
    fp_a, fm_a = join([fp_a, fm_a], one)
    gp_b, gm_b = hop("z", *join(ub[:2], fp_a))
    lo, hi = join([lo, hi], fp_a)
    sg_x = (both, one, lo, hi, three)
    bg_c = swap(tie(bg, lo), "c")
    tok = tokens_of(jnp.stack([x, h]), sg_x, so_x, d, tok_t.shape[1], 2 * rank)
    gp_b, gm_b, far_0 = join([gp_b, gm_b, far_0], tok)
    ap, am = relay(gp_b, gm_b, *ub[2:4])
    fp_b, fm_b = hop("z", ap, am)
    fars = [v for far in (far_0,) for v in (far, swap(far, "c"))]
    tok = tie(tok, am)
    tok_c = swap(tok, "c")
    gg = update(coeff, block, d, sg_x, [bg, bg_c, *fars], ap)
    fp_b, fm_b = join([fp_b, fm_b], gg[-1])
    gp_g, gm_g = hop("z", *gg[:2])
    keep, send = up_sums(
        (l == h).astype(jnp.int32).reshape(1), (ua[4], gp_a, gm_a, fp_a, fm_a), (ub[4], gp_b, gm_b, fp_b, fm_b)
    )
    sent = swap(send, "l")
    hidden = hidden_of(c.reshape(1), tok, tok_c, w_gate.T, w_up.T, bg, bu, gg[-1])
    gp_g, gm_g = join([gp_g, gm_g], hidden)
    ap, am = relay(gp_g, gm_g, *gg[2:4])
    fp_g, fm_g = hop("z", ap, am)
    at_c = c.reshape(1)
    gate_near, gate_far = gate_early(at_c, held[0], gg[4], gp_g, gm_g, ap)
    up_near, up_far = up_sum(keep, tie(sent, gate_near))
    new_up = renew(at_c, held[1], up_near, swap(up_far, "c"))
    fp_g, fm_g = join([fp_g, fm_g], gate_near)
    gate_near, gate_far = gate_late(gate_near, gate_far, fp_g, fm_g)
    new_gate = gate_rows(at_c, held[0], gate_near, swap(gate_far, "c"))
    return hidden.T, new_gate, new_up


def solution(mesh):
    fine = Mesh(mesh.devices.reshape(4, 2, 4, 2, 2), AXES)
    pop, mp = ("z", "l"), ("x", "h", "c")
    return jax.shard_map(
        local,
        mesh=fine,
        in_specs=(
            P(pop, mp),
            P(None, mp),
            P(None, mp),
            P(pop, None, mp),
            P(pop, None, mp),
            P(pop, None, mp),
            P(pop, None, mp),
            P(pop),
        ),
        out_specs=(P(pop, mp), P(pop, mp), P(pop, mp)),
        check_vma=False,
    )
```

```python
import functools

import jax
import jax.numpy as jnp
from jax import lax
from jax.experimental import pallas as pl
from jax.experimental.pallas import tpu as pltpu
from jax.sharding import Mesh
from jax.sharding import PartitionSpec as P

bf16 = jnp.bfloat16
f32 = jnp.float32
noise_scale = 0.5
AXES = ("z", "l", "x", "h", "c")
RING = 4
VMEM = 58 * 1024 * 1024
HINT = 1
NT = (((1,), (1,)), ((), ()))
TN = (((0,), (0,)), ((), ()))


def _call(kernel, name, flops=0, moved=0, **kw):
    return pl.pallas_call(
        kernel,
        name=name,
        compiler_params=pltpu.CompilerParams(vmem_limit_bytes=VMEM),
        cost_estimate=pl.CostEstimate(flops=flops // HINT, bytes_accessed=moved // HINT, transcendentals=0),
        **kw,
    )


def _any(n):
    return [pl.BlockSpec(memory_space=pl.ANY)] * n


FULL = pl.BlockSpec(memory_space=pltpu.VMEM)
SCALARS = pl.BlockSpec(memory_space=pltpu.SMEM)


def swap(v, axis, shift=1):
    n = lax.axis_size(axis)
    return lax.ppermute(v, axis, [(i, (i + shift) % n) for i in range(n)])


def join(vs, *after):
    n = len(vs)
    return _call(
        lambda *refs: None,
        "join",
        in_specs=_any(n + len(after)),
        out_specs=_any(n),
        out_shape=[jax.ShapeDtypeStruct(v.shape, v.dtype) for v in vs],
        input_output_aliases={i: i for i in range(n)},
    )(*vs, *after)


def tie(v, *after):
    return join([v], *after)[0]


def _own_mask(members, tokens):
    m = lax.broadcasted_iota(jnp.int32, (members, tokens), 0)
    t = lax.broadcasted_iota(jnp.int32, (members, tokens), 1)
    return jnp.logical_or(t == 2 * m, t == 2 * m + 1)


def _pack_kernel(tok_ref, ag_ref, au_ref, fit_ref, sg_ref, su_ref, all_ref):
    rank, d, m = ag_ref.shape
    tok = tok_ref[...]
    t = tok.shape[1]
    fit = fit_ref[...]
    mask = _own_mask(m, t)
    rows = []
    for a_ref, s_refs in ((ag_ref, (sg_ref,)), (au_ref, (su_ref, all_ref))):
        for r in range(rank):
            a = a_ref[r]
            for s_ref in s_refs:
                s_ref[r * d : (r + 1) * d, :] = (a.astype(f32) * fit).astype(bf16)
            s = lax.dot_general(a, tok, TN, preferred_element_type=f32)
            rows.append(jnp.sum(jnp.where(mask, s, 0.0), axis=0, keepdims=True))
    part = jnp.concatenate(rows, axis=0)
    high = part.astype(bf16)
    low = (part - high.astype(f32)).astype(bf16)
    at = rank * d
    for v in (tok, jnp.concatenate([high, low], axis=0)):
        for lo in range(0, t, m):
            all_ref[at : at + v.shape[0], :] = v[:, lo : lo + m]
            at += v.shape[0]


def pack(tok_t, ag, au, fit):
    rank, d, m = ag.shape
    t = tok_t.shape[1]
    pay = (d + 4 * rank) * (t // m)
    return _call(
        _pack_kernel,
        "pack",
        flops=4 * rank * d * m * t,
        moved=8 * rank * d * m,
        in_specs=[FULL] * 4,
        out_specs=[FULL] * 3,
        out_shape=[jax.ShapeDtypeStruct((n, m), bf16) for n in (rank * d, rank * d, rank * d + pay)],
    )(tok_t, ag, au, fit)


def _pick_kernel(y_ref, s_ref, pa_ref, pb_ref, all_ref, *refs):
    out_ref = refs[-1]
    n = s_ref.shape[0]
    y = y_ref[0]
    for where, at, ref in (
        (y == 1, 0, pb_ref),
        (y == 2, 0, pa_ref),
        (jnp.logical_or(y == 0, y == 3), 0, s_ref),
        (y < 2, n, pa_ref),
        (y >= 2, n, pb_ref),
    ):

        @pl.when(where)
        def _():
            out_ref[at : at + n, :] = ref[...]

    out_ref[2 * n :, :] = all_ref[n:, :]


def pick(y, s, pa, pb, rest, *after):
    n, m = s.shape
    return _call(
        _pick_kernel,
        "pick",
        moved=8 * s.size,
        in_specs=[SCALARS, FULL, FULL, FULL, FULL] + _any(len(after)),
        out_specs=FULL,
        out_shape=jax.ShapeDtypeStruct((n + rest.shape[0], m), s.dtype),
    )(y, s, pa, pb, rest, *after)


def rows_of(refs, lo, hi):
    if len(refs) == 1:
        return refs[0][lo:hi, :]
    n = refs[0].shape[0]
    parts = []
    if lo < n:
        parts.append(refs[0][lo : min(hi, n), :])
    if hi > n:
        parts.append(refs[1][max(lo, n) - n : hi - n, :])
    return parts[0] if len(parts) == 1 else jnp.concatenate(parts, axis=0)


def blocks_of(refs):
    own, one, two_lo, two_hi, three = refs
    return [own], [one], [two_lo, two_hi], [three]


PIECES = 5


ORDER = (2, 1, 3, 0)


def _update_kernel(coeff, slabs, d, rest, nb, nafter, block_ref, *refs):
    blocks = blocks_of(refs[:PIECES])
    b_refs = refs[PIECES : PIECES + nb]
    pp_ref, pm_ref, rp_ref, rm_ref, own_ref, lhs_ref, rhs_ref = refs[PIECES + nb + nafter :]
    m = b_refs[0].shape[2]
    n = d // 2
    i = pl.program_id(0)

    @pl.when(i == 0)
    def _():
        for step in range(RING):
            for j, block in enumerate(blocks):

                @pl.when(block_ref[step] == j)
                def _():
                    for k in range(slabs):
                        lhs_ref[step * d : (step + 1) * d, k * m : (k + 1) * m] = rows_of(block, k * d, (k + 1) * d)

    def put(acc):
        acc = (acc * coeff).astype(bf16)
        two, one, back, own = (acc[k * d : (k + 1) * d] for k in range(RING))
        w = acc.shape[1]
        pp_ref[:n, :w] = two[:n]
        pm_ref[:n, :w] = two[n:]
        pp_ref[n:, :w] = one[n:]
        rp_ref[:, :w] = one[:n]
        pm_ref[n:, :w] = back[:n]
        rm_ref[:, :w] = back[n:]
        own_ref[:, :w] = own

    slab = [(first, r) for first in range(0, nb, 2) for r in range(b_refs[first].shape[0])]
    for side in range(2):

        @pl.when(i == side)
        def _():
            for k, (first, r) in enumerate(slab):
                rhs_ref[:, k * m : (k + 1) * m] = b_refs[first + side][r]

    @pl.when(i < 2)
    def _():
        put(lax.dot_general(lhs_ref[...], rhs_ref[...], NT, preferred_element_type=f32))

    @pl.when(i == 2)
    def _():
        for k, (first, r) in enumerate(slab):
            for side in range(2):
                rhs_ref[side * rest : (side + 1) * rest, k * m : (k + 1) * m] = b_refs[first + side][r, :rest, :]
        put(lax.dot_general(lhs_ref[...], rhs_ref[: 2 * rest, :], NT, preferred_element_type=f32))


CUT = 1152


def update(coeff, block, rows, factors, seconds, *after):
    _, q, m = seconds[0].shape
    slabs = sum(b.shape[0] for b in seconds[::2])
    d = rows
    wide = 2 * q

    def once(shape):
        return pl.BlockSpec(shape, lambda i, w: (0,) * len(shape), pipeline_mode=pl.Buffered(1))

    def cut(n):
        return pl.BlockSpec((n, CUT), lambda i, w: (0, i))

    def near(b):
        return pl.BlockSpec((b.shape[0], CUT, m), lambda i, w: (0, jnp.minimum(i, 1), 0))

    def far(b):
        return pl.BlockSpec((b.shape[0], CUT, m), lambda i, w: (0, jnp.maximum(i - 1, 0), 0))

    sizes = (d, d, d // 2, d // 2, d)
    return _call(
        functools.partial(_update_kernel, coeff, slabs, d, q - CUT, len(seconds), len(after)),
        "update",
        flops=2 * RING * d * slabs * m * wide,
        moved=2 * (RING * slabs * d * m + slabs * m * wide + RING * d * wide),
        grid_spec=pltpu.PrefetchScalarGridSpec(
            num_scalar_prefetch=1,
            grid=(3,),
            in_specs=[once(f.shape) for f in factors] + [(near, far)[i % 2](b) for i, b in enumerate(seconds)] + _any(len(after)),
            out_specs=[cut(n) for n in sizes],
            scratch_shapes=[pltpu.VMEM((RING * d, slabs * m), bf16), pltpu.VMEM((CUT, slabs * m), bf16)],
        ),
        out_shape=[jax.ShapeDtypeStruct((n, wide), bf16) for n in sizes],
    )(block, *factors, *seconds, *after)


def _at(shape, row=0):
    return pl.BlockSpec(shape, lambda i: (row, 0))


WIDE = 1280


def _relay_kernel(gp_ref, gm_ref, rp_ref, rm_ref, *refs):
    ap_ref, am_ref = refs[-2:]
    ap_ref[...] = (rp_ref[...].astype(f32) + gp_ref[...].astype(f32)).astype(bf16)
    am_ref[...] = (rm_ref[...].astype(f32) + gm_ref[...].astype(f32)).astype(bf16)


def relay(gp, gm, rp, rm, *after):
    spec = pl.BlockSpec((rp.shape[0], WIDE), lambda i: (0, i))
    return _call(
        _relay_kernel,
        "relay",
        grid=(2,),
        moved=12 * rp.size,
        in_specs=[spec] * 4 + _any(len(after)),
        out_specs=[spec] * 2,
        out_shape=[jax.ShapeDtypeStruct(rp.shape, bf16)] * 2,
    )(gp, gm, rp, rm, *after)


def _halves_kernel(one_ref, three_ref, *refs):
    lo_ref, hi_ref = refs[-2:]
    lo_ref[...] = one_ref[...]
    hi_ref[...] = three_ref[...]


def halves(one, three, *after):
    n, m = one.shape[0] // 2, one.shape[1]
    return _call(
        _halves_kernel,
        "halves",
        grid=(1,),
        moved=8 * n * m,
        in_specs=[_at((n, m)), _at((n, m), 1)] + _any(len(after)),
        out_specs=[_at((n, m))] * 2,
        out_shape=[jax.ShapeDtypeStruct((n, m), bf16)] * 2,
    )(one, three, *after)


def _total(own_ref, gp_ref, gm_ref, fp_ref, fm_ref):
    n = fp_ref.shape[0]
    first = own_ref[:n, :].astype(f32) + gm_ref[n:, :].astype(f32) + fp_ref[...].astype(f32)
    second = own_ref[n:, :].astype(f32) + gp_ref[n:, :].astype(f32) + fm_ref[...].astype(f32)
    return jnp.concatenate([first, second], axis=0)


def _split(total, near_ref, far_ref):
    q, k = near_ref.shape[1], CUT
    near_ref[:, :k] = total[:, :k]
    near_ref[:, k:] = total[:, 2 * k : k + q]
    far_ref[:, :k] = total[:, k : 2 * k].astype(far_ref.dtype)
    far_ref[:, k:] = total[:, k + q :].astype(far_ref.dtype)


def _ends(shape):
    d, q = shape[0], shape[1] // 2
    return [jax.ShapeDtypeStruct((d, q), f32), jax.ShapeDtypeStruct((d, q), bf16)]


def _gate_early_kernel(c_ref, held_ref, own_ref, gp_ref, gm_ref, *refs):
    near_ref, far_ref = refs[-2:]
    d = own_ref.shape[0]
    n = d // 2
    first = own_ref[:n, :].astype(f32) + gm_ref[n:, :].astype(f32)
    second = own_ref[n:, :].astype(f32) + gp_ref[n:, :].astype(f32)
    _split(jnp.concatenate([first, second], axis=0), near_ref, far_ref)
    near_ref[...] += held_ref[pl.ds(pl.multiple_of(c_ref[0] * d, d), d), :].astype(f32)


def gate_early(c, held, own, gp, gm, *after):
    d, q = own.shape[0], own.shape[1] // 2
    return _call(
        _gate_early_kernel,
        "gate_early",
        in_specs=[SCALARS] + [FULL] * 4 + _any(len(after)),
        out_specs=[FULL] * 2,
        out_shape=[jax.ShapeDtypeStruct((d, q), f32)] * 2,
    )(c, held, own, gp, gm, *after)


def _gate_late_kernel(near_ref, far_ref, fp_ref, fm_ref, out_ref, send_ref):
    q, k = near_ref.shape[1], CUT
    for i, ref in enumerate((fp_ref, fm_ref)):

        @pl.when(pl.program_id(0) == i)
        def _():
            out_ref[:, :k] = (near_ref[:, :k] + ref[:, :k].astype(f32)).astype(bf16)
            out_ref[:, k:] = (near_ref[:, k:] + ref[:, 2 * k : k + q].astype(f32)).astype(bf16)
            send_ref[:, :k] = (far_ref[:, :k] + ref[:, k : 2 * k].astype(f32)).astype(bf16)
            send_ref[:, k:] = (far_ref[:, k:] + ref[:, k + q :].astype(f32)).astype(bf16)


def gate_late(near, far, fp, fm):
    n, wide = fp.shape
    half = pl.BlockSpec((n, near.shape[1]), lambda i: (i, 0))
    whole = pl.BlockSpec((n, wide), lambda i: (0, 0))
    return _call(
        _gate_late_kernel,
        "gate_late",
        grid=(2,),
        in_specs=[half, half, whole, whole],
        out_specs=[half, half],
        out_shape=[jax.ShapeDtypeStruct(near.shape, bf16)] * 2,
    )(near, far, fp, fm)


def _gate_rows_kernel(c_ref, held_ref, near_ref, far_ref, out_ref):
    mine = pl.program_id(0) == c_ref[0]

    @pl.when(mine)
    def _():
        out_ref[...] = near_ref[...]

    @pl.when(jnp.logical_not(mine))
    def _():
        out_ref[...] = (held_ref[...].astype(f32) + far_ref[...].astype(f32)).astype(bf16)


def gate_rows(c, held, near, far):
    part = pl.BlockSpec(near.shape, lambda i: (i, 0))
    all_of = pl.BlockSpec(near.shape, lambda i: (0, 0))
    return _call(
        _gate_rows_kernel,
        "gate_rows",
        grid=(2,),
        in_specs=[SCALARS, part, all_of, all_of],
        out_specs=part,
        out_shape=jax.ShapeDtypeStruct(held.shape, bf16),
    )(c, held, near, far)


def _up_sums_kernel(mine_ref, *refs):
    keep_ref, send_ref = refs[10:]
    a, b = _total(*refs[:5]), _total(*refs[5:10])
    mine = mine_ref[0] == 1
    keep_ref[...] = jnp.where(mine, a, b)
    send_ref[...] = jnp.where(mine, b, a).astype(bf16)


def up_sums(mine, parts_a, parts_b, *after):
    shape = parts_a[0].shape

    def kernel(mine_ref, *refs):
        _up_sums_kernel(mine_ref, *refs[:10], *refs[-2:])

    return _call(
        kernel,
        "up_sums",
        grid=(2,),
        in_specs=[SCALARS] + [pl.BlockSpec((p.shape[0], WIDE), lambda i: (0, i)) for p in (*parts_a, *parts_b)] + _any(len(after)),
        out_specs=[pl.BlockSpec((shape[0], WIDE), lambda i: (0, i))] * 2,
        out_shape=[jax.ShapeDtypeStruct(shape, f32), jax.ShapeDtypeStruct(shape, bf16)],
    )(mine, *parts_a, *parts_b, *after)


def up_sum(keep, sent):
    def kernel(keep_ref, sent_ref, near_ref, far_ref):
        _split(keep_ref[...] + sent_ref[...].astype(f32), near_ref, far_ref)

    return _call(
        kernel,
        "up_sum",
        in_specs=[FULL] * 2,
        out_specs=[FULL] * 2,
        out_shape=_ends(keep.shape),
    )(keep, sent)


def _renew_kernel(c_ref, held_ref, near_ref, far_ref, out_ref):
    d = near_ref.shape[0]
    near, far = near_ref[...], far_ref[...].astype(f32)

    def put(first, second):
        out_ref[:d, :] = (held_ref[:d, :].astype(f32) + first).astype(bf16)
        out_ref[d:, :] = (held_ref[d:, :].astype(f32) + second).astype(bf16)

    @pl.when(c_ref[0] == 0)
    def _():
        put(near, far)

    @pl.when(c_ref[0] == 1)
    def _():
        put(far, near)


def renew(c, held, near, far):
    return _call(
        _renew_kernel,
        "renew",
        in_specs=[SCALARS] + [FULL] * 3,
        out_specs=FULL,
        out_shape=jax.ShapeDtypeStruct(held.shape, bf16),
    )(c, held, near, far)


def _tokens_kernel(n, at_ref, *refs):
    tok_ref = refs[-1]
    t, m = tok_ref.shape[1], refs[0].shape[1]
    d = (tok_ref.shape[0] - 2 * n) // (2 * RING)
    x, h = at_ref[0], at_ref[1]
    wide = t // m
    total = None
    for s in range(2):
        gather = refs[s * PIECES : (s + 1) * PIECES]
        start = gather[0].shape[0] - wide * (d + 2 * n)
        for j, block in enumerate(blocks_of(gather)):
            rows = [rows_of(block, start + i * d, start + (i + 1) * d) for i in range(wide)]
            to = 2 * lax.rem(x + RING - j, RING) + (h if s == 0 else 1 - h)
            tok_ref[pl.ds(pl.multiple_of(to * d, d), d), :] = jnp.concatenate(rows, axis=1)
            at = start + wide * d
            terms = [rows_of(block, at + i * 2 * n, at + (i + 1) * 2 * n).astype(f32) for i in range(wide)]
            both = jnp.concatenate(terms, axis=1)
            value = both[:n] + both[n:]
            total = value if total is None else total + value
    high = total.astype(bf16)
    low = (total - high.astype(f32)).astype(bf16)
    tok_ref[2 * RING * d :, :] = jnp.concatenate([high, low], axis=0)


def tokens_of(at, own, other, d, t, probes, *after):
    return _call(
        functools.partial(_tokens_kernel, probes),
        "tokens",
        moved=8 * RING * 2 * d * t,
        in_specs=[SCALARS] + [FULL] * (2 * PIECES) + _any(len(after)),
        out_specs=FULL,
        out_shape=jax.ShapeDtypeStruct((2 * RING * d + 2 * probes, t), bf16),
    )(at, *own, *other, *after)


def _hidden_kernel(c_ref, mine_ref, other_ref, wg_ref, wu_ref, bg_ref, bu_ref, *refs):
    out_ref, tok_ref, p_ref = refs[-3:]
    rank, _, m = bg_ref.shape
    t = mine_ref.shape[1]
    n = 2 * rank
    d = (mine_ref.shape[0] - 2 * n) // (2 * RING)

    @pl.when(pl.program_id(0) == 0)
    def _():
        c = c_ref[0]
        for ref, core in ((mine_ref, c), (other_ref, 1 - c)):
            for i in range(2 * RING):
                tok_ref[pl.ds(pl.multiple_of((2 * i + core) * d, d), d), :] = ref[i * d : (i + 1) * d, :]
        mask = _own_mask(m, t)
        terms = mine_ref[2 * RING * d :, :].astype(f32) + other_ref[2 * RING * d :, :].astype(f32)
        probe = (terms[:n] + terms[n:]).astype(bf16).astype(f32) * noise_scale
        for i in range(2 * rank):
            row = jnp.broadcast_to(probe[i : i + 1, :], (m, t))
            p_ref[i * m : (i + 1) * m, :] = jnp.where(mask, row, 0.0).astype(bf16)

    pre = []
    for k, (w_ref, b_ref) in enumerate(((wg_ref, bg_ref), (wu_ref, bu_ref))):
        b = jnp.concatenate([b_ref[r] for r in range(rank)], axis=1)
        acc = jnp.dot(w_ref[...], tok_ref[...], preferred_element_type=f32)
        acc += jnp.dot(b, p_ref[k * rank * m : (k + 1) * rank * m, :], preferred_element_type=f32)
        pre.append(acc)
    g, u = pre
    out_ref[...] = (g / (1.0 + jnp.exp(-g)) * u).astype(out_ref.dtype)


def hidden_of(c, mine, other, wg, wu, bg, bu, *after):
    t = mine.shape[1]
    q, d = wg.shape
    rank, _, m = bg.shape
    block = 304
    w_spec = pl.BlockSpec((block, d), lambda i: (i, 0))
    b_spec = pl.BlockSpec((rank, block, m), lambda i: (0, i, 0))
    t_spec = pl.BlockSpec(mine.shape, lambda i: (0, 0), pipeline_mode=pl.Buffered(1))
    return _call(
        _hidden_kernel,
        "hidden",
        flops=4 * q * t * (d + rank * m),
        moved=2 * (2 * q * d + d * t + 2 * rank * q * m + q * t),
        grid=(pl.cdiv(q, block),),
        in_specs=[SCALARS, t_spec, t_spec, w_spec, w_spec, b_spec, b_spec] + _any(len(after)),
        out_specs=pl.BlockSpec((block, t), lambda i: (i, 0)),
        out_shape=jax.ShapeDtypeStruct((q, t), bf16),
        scratch_shapes=[pltpu.VMEM((d, t), bf16), pltpu.VMEM((2 * rank * m, t), bf16)],
    )(c, mine, other, wg, wu, bg, bu, *after)


def local(tokens, w_gate, w_up, a_gate, a_up, b_gate, b_up, fitness):
    members, rank, d = a_gate.shape
    q = w_gate.shape[1]
    coeff = 1.0 / (members * lax.axis_size("z") * lax.axis_size("l") * rank) ** 0.5
    z, l, x, h, c = (lax.axis_index(a) for a in AXES)
    tok_t = tokens.T
    ag_t, au_t = (a.transpose(1, 2, 0) for a in (a_gate, a_up))
    bg, bu = (b.transpose(1, 2, 0) for b in (b_gate, b_up))
    block = (x - z - jnp.array(ORDER, jnp.int32)) % RING

    sg, su, rest = pack(tok_t, ag_t, au_t, fitness[None, :])
    bu_c = swap(bu, "c")

    def hop(axis, first, second):
        return swap(first, axis, 1), swap(second, axis, -1)

    one, three = hop("x", su, su)
    first = (2 * z + l) * 2 * d
    held = [lax.dynamic_slice_in_dim(w, first, 2 * d, 0) for w in (w_gate, w_up)]
    so = swap(rest, "h")
    one, three, bu_c, *held = join([one, three, bu_c, *held])
    at_y = (0, 2, 1, 3)
    sg_y = tie(sg, so)
    pa, pb = (
        lax.ppermute(sg_y, ("l", "h"), [(at_y[i], at_y[j]) for i, j in pairs])
        for pairs in (((1, 0), (2, 1), (0, 2)), ((3, 1), (1, 2), (2, 3)))
    )
    lo, hi, so = join([*hop("x", *halves(one, three)), so])
    su_x = (su, one, lo, hi, three)
    so = tie(so, lo)
    one, three = hop("x", so, so)
    ua = update(coeff, block, d, su_x, [bu, bu_c], so)
    gp_a, gm_a = hop("z", *ua[:2])
    one, three, pb = join([one, three, pb], ua[-1])
    lo, hi = hop("x", *halves(one, three))
    both = pick((2 * h + l).reshape(1), sg_y, pa, pb, rest, one)
    far_0 = swap(tie(bg, both), "l")
    lo, hi = join([lo, hi], both)
    so_x = (so, one, lo, hi, three)
    both = tie(both, lo)
    one, three = hop("x", both, both)
    gp_a, gm_a = join([gp_a, gm_a], both)
    ap, am = relay(gp_a, gm_a, *ua[2:4])
    fp_a, fm_a = hop("z", ap, am)
    ub = update(coeff, block, d, so_x, [bu, bu_c], ap)
    one, three = join([one, three], ap, ub[-1])
    lo, hi = hop("x", *halves(one, three))
    fp_a, fm_a = join([fp_a, fm_a], one)
    gp_b, gm_b = hop("z", *join(ub[:2], fp_a))
    lo, hi = join([lo, hi], fp_a)
    sg_x = (both, one, lo, hi, three)
    bg_c = swap(tie(bg, lo), "c")
    tok = tokens_of(jnp.stack([x, h]), sg_x, so_x, d, tok_t.shape[1], 2 * rank)
    gp_b, gm_b, far_0 = join([gp_b, gm_b, far_0], tok)
    ap, am = relay(gp_b, gm_b, *ub[2:4])
    fp_b, fm_b = hop("z", ap, am)
    fars = [v for far in (far_0,) for v in (far, swap(far, "c"))]
    tok = tie(tok, am)
    tok_c = swap(tok, "c")
    gg = update(coeff, block, d, sg_x, [bg, bg_c, *fars], ap)
    fp_b, fm_b = join([fp_b, fm_b], gg[-1])
    gp_g, gm_g = hop("z", *gg[:2])
    keep, send = up_sums(
        (l == h).astype(jnp.int32).reshape(1), (ua[4], gp_a, gm_a, fp_a, fm_a), (ub[4], gp_b, gm_b, fp_b, fm_b)
    )
    sent = swap(send, "l")
    hidden = hidden_of(c.reshape(1), tok, tok_c, w_gate.T, w_up.T, bg, bu, gg[-1])
    gp_g, gm_g = join([gp_g, gm_g], hidden)
    ap, am = relay(gp_g, gm_g, *gg[2:4])
    fp_g, fm_g = hop("z", ap, am)
    at_c = c.reshape(1)
    gate_near, gate_far = gate_early(at_c, held[0], gg[4], gp_g, gm_g, ap)
    up_near, up_far = up_sum(keep, tie(sent, gate_near))
    new_up = renew(at_c, held[1], up_near, swap(up_far, "c"))
    fp_g, fm_g = join([fp_g, fm_g], gate_near)
    gate_near, gate_far = gate_late(gate_near, gate_far, fp_g, fm_g)
    new_gate = gate_rows(at_c, held[0], gate_near, swap(gate_far, "c"))
    return hidden.T, new_gate, new_up


def solution(mesh):
    fine = Mesh(mesh.devices.reshape(4, 2, 4, 2, 2), AXES)
    pop, mp = ("z", "l"), ("x", "h", "c")
    return jax.shard_map(
        local,
        mesh=fine,
        in_specs=(
            P(pop, mp),
            P(None, mp),
            P(None, mp),
            P(pop, None, mp),
            P(pop, None, mp),
            P(pop, None, mp),
            P(pop, None, mp),
            P(pop),
        ),
        out_specs=(P(pop, mp), P(pop, mp), P(pop, mp)),
        check_vma=False,
    )
```

```python
import functools

import jax
import jax.numpy as jnp
from jax import lax
from jax.experimental import pallas as pl
from jax.experimental.pallas import tpu as pltpu
from jax.sharding import Mesh
from jax.sharding import PartitionSpec as P

bf16 = jnp.bfloat16
f32 = jnp.float32
noise_scale = 0.5
AXES = ("z", "l", "x", "h", "c")
RING = 4
VMEM = 58 * 1024 * 1024
HINT = 1
NT = (((1,), (1,)), ((), ()))
TN = (((0,), (0,)), ((), ()))


def _call(kernel, name, flops=0, moved=0, **kw):
    return pl.pallas_call(
        kernel,
        name=name,
        compiler_params=pltpu.CompilerParams(vmem_limit_bytes=VMEM),
        cost_estimate=pl.CostEstimate(flops=flops // HINT, bytes_accessed=moved // HINT, transcendentals=0),
        **kw,
    )


def _any(n):
    return [pl.BlockSpec(memory_space=pl.ANY)] * n


FULL = pl.BlockSpec(memory_space=pltpu.VMEM)
SCALARS = pl.BlockSpec(memory_space=pltpu.SMEM)


def swap(v, axis, shift=1):
    n = lax.axis_size(axis)
    return lax.ppermute(v, axis, [(i, (i + shift) % n) for i in range(n)])


def join(vs, *after):
    n = len(vs)
    return _call(
        lambda *refs: None,
        "join",
        in_specs=_any(n + len(after)),
        out_specs=_any(n),
        out_shape=[jax.ShapeDtypeStruct(v.shape, v.dtype) for v in vs],
        input_output_aliases={i: i for i in range(n)},
    )(*vs, *after)


def tie(v, *after):
    return join([v], *after)[0]


def _own_mask(members, tokens):
    m = lax.broadcasted_iota(jnp.int32, (members, tokens), 0)
    t = lax.broadcasted_iota(jnp.int32, (members, tokens), 1)
    return jnp.logical_or(t == 2 * m, t == 2 * m + 1)


def _pack_kernel(tok_ref, ag_ref, au_ref, fit_ref, sg_ref, su_ref, all_ref):
    rank, d, m = ag_ref.shape
    tok = tok_ref[...]
    t = tok.shape[1]
    fit = fit_ref[...]
    mask = _own_mask(m, t)
    rows = []
    for a_ref, s_refs in ((ag_ref, (sg_ref,)), (au_ref, (su_ref, all_ref))):
        for r in range(rank):
            a = a_ref[r]
            for s_ref in s_refs:
                s_ref[r * d : (r + 1) * d, :] = (a.astype(f32) * fit).astype(bf16)
            s = lax.dot_general(a, tok, TN, preferred_element_type=f32)
            rows.append(jnp.sum(jnp.where(mask, s, 0.0), axis=0, keepdims=True))
    part = jnp.concatenate(rows, axis=0)
    high = part.astype(bf16)
    low = (part - high.astype(f32)).astype(bf16)
    at = rank * d
    for v in (tok, jnp.concatenate([high, low], axis=0)):
        for lo in range(0, t, m):
            all_ref[at : at + v.shape[0], :] = v[:, lo : lo + m]
            at += v.shape[0]


def pack(tok_t, ag, au, fit):
    rank, d, m = ag.shape
    t = tok_t.shape[1]
    pay = (d + 4 * rank) * (t // m)
    return _call(
        _pack_kernel,
        "pack",
        flops=4 * rank * d * m * t,
        moved=8 * rank * d * m,
        in_specs=[FULL] * 4,
        out_specs=[FULL] * 3,
        out_shape=[jax.ShapeDtypeStruct((n, m), bf16) for n in (rank * d, rank * d, rank * d + pay)],
    )(tok_t, ag, au, fit)


def _pick_kernel(y_ref, s_ref, pa_ref, pb_ref, all_ref, *refs):
    out_ref = refs[-1]
    n = s_ref.shape[0]
    y = y_ref[0]
    for where, at, ref in (
        (y == 1, 0, pb_ref),
        (y == 2, 0, pa_ref),
        (jnp.logical_or(y == 0, y == 3), 0, s_ref),
        (y < 2, n, pa_ref),
        (y >= 2, n, pb_ref),
    ):

        @pl.when(where)
        def _():
            out_ref[at : at + n, :] = ref[...]

    out_ref[2 * n :, :] = all_ref[n:, :]


def pick(y, s, pa, pb, rest, *after):
    n, m = s.shape
    return _call(
        _pick_kernel,
        "pick",
        moved=8 * s.size,
        in_specs=[SCALARS, FULL, FULL, FULL, FULL] + _any(len(after)),
        out_specs=FULL,
        out_shape=jax.ShapeDtypeStruct((n + rest.shape[0], m), s.dtype),
    )(y, s, pa, pb, rest, *after)


def rows_of(refs, lo, hi):
    if len(refs) == 1:
        return refs[0][lo:hi, :]
    n = refs[0].shape[0]
    parts = []
    if lo < n:
        parts.append(refs[0][lo : min(hi, n), :])
    if hi > n:
        parts.append(refs[1][max(lo, n) - n : hi - n, :])
    return parts[0] if len(parts) == 1 else jnp.concatenate(parts, axis=0)


def blocks_of(refs):
    own, one, two_lo, two_hi, three = refs
    return [own], [one], [two_lo, two_hi], [three]


PIECES = 5


ORDER = (2, 1, 3, 0)


def _update_kernel(coeff, slabs, d, rest, nb, nafter, block_ref, *refs):
    blocks = blocks_of(refs[:PIECES])
    b_refs = refs[PIECES : PIECES + nb]
    pp_ref, pm_ref, rp_ref, rm_ref, own_ref, lhs_ref, rhs_ref = refs[PIECES + nb + nafter :]
    m = b_refs[0].shape[2]
    n = d // 2
    i = pl.program_id(0)

    @pl.when(i == 0)
    def _():
        for step in range(RING):
            for j, block in enumerate(blocks):

                @pl.when(block_ref[step] == j)
                def _():
                    for k in range(slabs):
                        lhs_ref[step * d : (step + 1) * d, k * m : (k + 1) * m] = rows_of(block, k * d, (k + 1) * d)

    def put(acc):
        acc = (acc * coeff).astype(bf16)
        two, one, back, own = (acc[k * d : (k + 1) * d] for k in range(RING))
        w = acc.shape[1]
        pp_ref[:n, :w] = two[:n]
        pm_ref[:n, :w] = two[n:]
        pp_ref[n:, :w] = one[n:]
        rp_ref[:, :w] = one[:n]
        pm_ref[n:, :w] = back[:n]
        rm_ref[:, :w] = back[n:]
        own_ref[:, :w] = own

    slab = [(first, r) for first in range(0, nb, 2) for r in range(b_refs[first].shape[0])]
    for side in range(2):

        @pl.when(i == side)
        def _():
            for k, (first, r) in enumerate(slab):
                rhs_ref[:, k * m : (k + 1) * m] = b_refs[first + side][r]

    @pl.when(i < 2)
    def _():
        put(lax.dot_general(lhs_ref[...], rhs_ref[...], NT, preferred_element_type=f32))

    @pl.when(i == 2)
    def _():
        for k, (first, r) in enumerate(slab):
            for side in range(2):
                rhs_ref[side * rest : (side + 1) * rest, k * m : (k + 1) * m] = b_refs[first + side][r, :rest, :]
        put(lax.dot_general(lhs_ref[...], rhs_ref[: 2 * rest, :], NT, preferred_element_type=f32))


CUT = 1152


def update(coeff, block, rows, factors, seconds, *after):
    _, q, m = seconds[0].shape
    slabs = sum(b.shape[0] for b in seconds[::2])
    d = rows
    wide = 2 * q

    def once(shape):
        return pl.BlockSpec(shape, lambda i, w: (0,) * len(shape), pipeline_mode=pl.Buffered(1))

    def cut(n):
        return pl.BlockSpec((n, CUT), lambda i, w: (0, i))

    def near(b):
        return pl.BlockSpec((b.shape[0], CUT, m), lambda i, w: (0, jnp.minimum(i, 1), 0))

    def far(b):
        return pl.BlockSpec((b.shape[0], CUT, m), lambda i, w: (0, jnp.maximum(i - 1, 0), 0))

    sizes = (d, d, d // 2, d // 2, d)
    return _call(
        functools.partial(_update_kernel, coeff, slabs, d, q - CUT, len(seconds), len(after)),
        "update",
        flops=2 * RING * d * slabs * m * wide,
        moved=2 * (RING * slabs * d * m + slabs * m * wide + RING * d * wide),
        grid_spec=pltpu.PrefetchScalarGridSpec(
            num_scalar_prefetch=1,
            grid=(3,),
            in_specs=[once(f.shape) for f in factors] + [(near, far)[i % 2](b) for i, b in enumerate(seconds)] + _any(len(after)),
            out_specs=[cut(n) for n in sizes],
            scratch_shapes=[pltpu.VMEM((RING * d, slabs * m), bf16), pltpu.VMEM((CUT, slabs * m), bf16)],
        ),
        out_shape=[jax.ShapeDtypeStruct((n, wide), bf16) for n in sizes],
    )(block, *factors, *seconds, *after)


def _at(shape, row=0):
    return pl.BlockSpec(shape, lambda i: (row, 0))


WIDE = 1280


def _relay_kernel(gp_ref, gm_ref, rp_ref, rm_ref, *refs):
    ap_ref, am_ref = refs[-2:]
    ap_ref[...] = (rp_ref[...].astype(f32) + gp_ref[...].astype(f32)).astype(bf16)
    am_ref[...] = (rm_ref[...].astype(f32) + gm_ref[...].astype(f32)).astype(bf16)


def relay(gp, gm, rp, rm, *after):
    spec = pl.BlockSpec((rp.shape[0], WIDE), lambda i: (0, i))
    return _call(
        _relay_kernel,
        "relay",
        grid=(2,),
        moved=12 * rp.size,
        in_specs=[spec] * 4 + _any(len(after)),
        out_specs=[spec] * 2,
        out_shape=[jax.ShapeDtypeStruct(rp.shape, bf16)] * 2,
    )(gp, gm, rp, rm, *after)


def _halves_kernel(one_ref, three_ref, *refs):
    lo_ref, hi_ref = refs[-2:]
    lo_ref[...] = one_ref[...]
    hi_ref[...] = three_ref[...]


def halves(one, three, *after):
    n, m = one.shape[0] // 2, one.shape[1]
    return _call(
        _halves_kernel,
        "halves",
        grid=(1,),
        moved=8 * n * m,
        in_specs=[_at((n, m)), _at((n, m), 1)] + _any(len(after)),
        out_specs=[_at((n, m))] * 2,
        out_shape=[jax.ShapeDtypeStruct((n, m), bf16)] * 2,
    )(one, three, *after)


def _total(own_ref, gp_ref, gm_ref, fp_ref, fm_ref):
    n = fp_ref.shape[0]
    first = own_ref[:n, :].astype(f32) + gm_ref[n:, :].astype(f32) + fp_ref[...].astype(f32)
    second = own_ref[n:, :].astype(f32) + gp_ref[n:, :].astype(f32) + fm_ref[...].astype(f32)
    return jnp.concatenate([first, second], axis=0)


def _split(total, near_ref, far_ref):
    q, k = near_ref.shape[1], CUT
    near_ref[:, :k] = total[:, :k]
    near_ref[:, k:] = total[:, 2 * k : k + q]
    far_ref[:, :k] = total[:, k : 2 * k].astype(far_ref.dtype)
    far_ref[:, k:] = total[:, k + q :].astype(far_ref.dtype)


def _ends(shape):
    d, q = shape[0], shape[1] // 2
    return [jax.ShapeDtypeStruct((d, q), f32), jax.ShapeDtypeStruct((d, q), bf16)]


def _gate_early_kernel(c_ref, held_ref, own_ref, gp_ref, gm_ref, *refs):
    near_ref, far_ref = refs[-2:]
    d = own_ref.shape[0]
    n = d // 2
    first = own_ref[:n, :].astype(f32) + gm_ref[n:, :].astype(f32)
    second = own_ref[n:, :].astype(f32) + gp_ref[n:, :].astype(f32)
    _split(jnp.concatenate([first, second], axis=0), near_ref, far_ref)
    near_ref[...] += held_ref[pl.ds(pl.multiple_of(c_ref[0] * d, d), d), :].astype(f32)


def gate_early(c, held, own, gp, gm, *after):
    d, q = own.shape[0], own.shape[1] // 2
    return _call(
        _gate_early_kernel,
        "gate_early",
        in_specs=[SCALARS] + [FULL] * 4 + _any(len(after)),
        out_specs=[FULL] * 2,
        out_shape=[jax.ShapeDtypeStruct((d, q), f32)] * 2,
    )(c, held, own, gp, gm, *after)


def _gate_late_kernel(near_ref, far_ref, fp_ref, fm_ref, out_ref, send_ref):
    q, k = near_ref.shape[1], CUT
    for i, ref in enumerate((fp_ref, fm_ref)):

        @pl.when(pl.program_id(0) == i)
        def _():
            out_ref[:, :k] = (near_ref[:, :k] + ref[:, :k].astype(f32)).astype(bf16)
            out_ref[:, k:] = (near_ref[:, k:] + ref[:, 2 * k : k + q].astype(f32)).astype(bf16)
            send_ref[:, :k] = (far_ref[:, :k] + ref[:, k : 2 * k].astype(f32)).astype(bf16)
            send_ref[:, k:] = (far_ref[:, k:] + ref[:, k + q :].astype(f32)).astype(bf16)


def gate_late(near, far, fp, fm):
    n, wide = fp.shape
    half = pl.BlockSpec((n, near.shape[1]), lambda i: (i, 0))
    whole = pl.BlockSpec((n, wide), lambda i: (0, 0))
    return _call(
        _gate_late_kernel,
        "gate_late",
        grid=(2,),
        in_specs=[half, half, whole, whole],
        out_specs=[half, half],
        out_shape=[jax.ShapeDtypeStruct(near.shape, bf16)] * 2,
    )(near, far, fp, fm)


def _gate_rows_kernel(c_ref, held_ref, near_ref, far_ref, out_ref):
    mine = pl.program_id(0) == c_ref[0]

    @pl.when(mine)
    def _():
        out_ref[...] = near_ref[...]

    @pl.when(jnp.logical_not(mine))
    def _():
        out_ref[...] = (held_ref[...].astype(f32) + far_ref[...].astype(f32)).astype(bf16)


def gate_rows(c, held, near, far):
    part = pl.BlockSpec(near.shape, lambda i: (i, 0))
    all_of = pl.BlockSpec(near.shape, lambda i: (0, 0))
    return _call(
        _gate_rows_kernel,
        "gate_rows",
        grid=(2,),
        in_specs=[SCALARS, part, all_of, all_of],
        out_specs=part,
        out_shape=jax.ShapeDtypeStruct(held.shape, bf16),
    )(c, held, near, far)


def _up_sums_kernel(mine_ref, *refs):
    keep_ref, send_ref = refs[10:]
    a, b = _total(*refs[:5]), _total(*refs[5:10])
    mine = mine_ref[0] == 1
    keep_ref[...] = jnp.where(mine, a, b)
    send_ref[...] = jnp.where(mine, b, a).astype(bf16)


def up_sums(mine, parts_a, parts_b, *after):
    shape = parts_a[0].shape

    def kernel(mine_ref, *refs):
        _up_sums_kernel(mine_ref, *refs[:10], *refs[-2:])

    return _call(
        kernel,
        "up_sums",
        grid=(2,),
        in_specs=[SCALARS] + [pl.BlockSpec((p.shape[0], WIDE), lambda i: (0, i)) for p in (*parts_a, *parts_b)] + _any(len(after)),
        out_specs=[pl.BlockSpec((shape[0], WIDE), lambda i: (0, i))] * 2,
        out_shape=[jax.ShapeDtypeStruct(shape, f32), jax.ShapeDtypeStruct(shape, bf16)],
    )(mine, *parts_a, *parts_b, *after)


def up_sum(keep, sent):
    def kernel(keep_ref, sent_ref, near_ref, far_ref):
        _split(keep_ref[...] + sent_ref[...].astype(f32), near_ref, far_ref)

    return _call(
        kernel,
        "up_sum",
        in_specs=[FULL] * 2,
        out_specs=[FULL] * 2,
        out_shape=_ends(keep.shape),
    )(keep, sent)


def _renew_kernel(c_ref, held_ref, near_ref, far_ref, out_ref):
    d = near_ref.shape[0]
    near, far = near_ref[...], far_ref[...].astype(f32)

    def put(first, second):
        out_ref[:d, :] = (held_ref[:d, :].astype(f32) + first).astype(bf16)
        out_ref[d:, :] = (held_ref[d:, :].astype(f32) + second).astype(bf16)

    @pl.when(c_ref[0] == 0)
    def _():
        put(near, far)

    @pl.when(c_ref[0] == 1)
    def _():
        put(far, near)


def renew(c, held, near, far):
    return _call(
        _renew_kernel,
        "renew",
        in_specs=[SCALARS] + [FULL] * 3,
        out_specs=FULL,
        out_shape=jax.ShapeDtypeStruct(held.shape, bf16),
    )(c, held, near, far)


def _tokens_kernel(n, at_ref, *refs):
    tok_ref = refs[-1]
    t, m = tok_ref.shape[1], refs[0].shape[1]
    d = (tok_ref.shape[0] - 2 * n) // (2 * RING)
    x, h = at_ref[0], at_ref[1]
    wide = t // m
    total = None
    for s in range(2):
        gather = refs[s * PIECES : (s + 1) * PIECES]
        start = gather[0].shape[0] - wide * (d + 2 * n)
        for j, block in enumerate(blocks_of(gather)):
            rows = [rows_of(block, start + i * d, start + (i + 1) * d) for i in range(wide)]
            to = 2 * lax.rem(x + RING - j, RING) + (h if s == 0 else 1 - h)
            tok_ref[pl.ds(pl.multiple_of(to * d, d), d), :] = jnp.concatenate(rows, axis=1)
            at = start + wide * d
            terms = [rows_of(block, at + i * 2 * n, at + (i + 1) * 2 * n).astype(f32) for i in range(wide)]
            both = jnp.concatenate(terms, axis=1)
            value = both[:n] + both[n:]
            total = value if total is None else total + value
    high = total.astype(bf16)
    low = (total - high.astype(f32)).astype(bf16)
    tok_ref[2 * RING * d :, :] = jnp.concatenate([high, low], axis=0)


def tokens_of(at, own, other, d, t, probes, *after):
    return _call(
        functools.partial(_tokens_kernel, probes),
        "tokens",
        moved=8 * RING * 2 * d * t,
        in_specs=[SCALARS] + [FULL] * (2 * PIECES) + _any(len(after)),
        out_specs=FULL,
        out_shape=jax.ShapeDtypeStruct((2 * RING * d + 2 * probes, t), bf16),
    )(at, *own, *other, *after)


def _hidden_kernel(c_ref, mine_ref, other_ref, wg_ref, wu_ref, bg_ref, bu_ref, *refs):
    out_ref, tok_ref, p_ref = refs[-3:]
    rank, _, m = bg_ref.shape
    t = mine_ref.shape[1]
    n = 2 * rank
    d = (mine_ref.shape[0] - 2 * n) // (2 * RING)

    @pl.when(pl.program_id(0) == 0)
    def _():
        c = c_ref[0]
        for ref, core in ((mine_ref, c), (other_ref, 1 - c)):
            for i in range(2 * RING):
                tok_ref[pl.ds(pl.multiple_of((2 * i + core) * d, d), d), :] = ref[i * d : (i + 1) * d, :]
        mask = _own_mask(m, t)
        terms = mine_ref[2 * RING * d :, :].astype(f32) + other_ref[2 * RING * d :, :].astype(f32)
        probe = (terms[:n] + terms[n:]).astype(bf16).astype(f32) * noise_scale
        for i in range(2 * rank):
            row = jnp.broadcast_to(probe[i : i + 1, :], (m, t))
            p_ref[i * m : (i + 1) * m, :] = jnp.where(mask, row, 0.0).astype(bf16)

    pre = []
    for k, (w_ref, b_ref) in enumerate(((wg_ref, bg_ref), (wu_ref, bu_ref))):
        b = jnp.concatenate([b_ref[r] for r in range(rank)], axis=1)
        acc = jnp.dot(w_ref[...], tok_ref[...], preferred_element_type=f32)
        acc += jnp.dot(b, p_ref[k * rank * m : (k + 1) * rank * m, :], preferred_element_type=f32)
        pre.append(acc)
    g, u = pre
    out_ref[...] = (g / (1.0 + jnp.exp(-g)) * u).astype(out_ref.dtype)


def hidden_of(c, mine, other, wg, wu, bg, bu, *after):
    t = mine.shape[1]
    q, d = wg.shape
    rank, _, m = bg.shape
    block = 240
    w_spec = pl.BlockSpec((block, d), lambda i: (i, 0))
    b_spec = pl.BlockSpec((rank, block, m), lambda i: (0, i, 0))
    t_spec = pl.BlockSpec(mine.shape, lambda i: (0, 0), pipeline_mode=pl.Buffered(1))
    return _call(
        _hidden_kernel,
        "hidden",
        flops=4 * q * t * (d + rank * m),
        moved=2 * (2 * q * d + d * t + 2 * rank * q * m + q * t),
        grid=(pl.cdiv(q, block),),
        in_specs=[SCALARS, t_spec, t_spec, w_spec, w_spec, b_spec, b_spec] + _any(len(after)),
        out_specs=pl.BlockSpec((block, t), lambda i: (i, 0)),
        out_shape=jax.ShapeDtypeStruct((q, t), bf16),
        scratch_shapes=[pltpu.VMEM((d, t), bf16), pltpu.VMEM((2 * rank * m, t), bf16)],
    )(c, mine, other, wg, wu, bg, bu, *after)


def local(tokens, w_gate, w_up, a_gate, a_up, b_gate, b_up, fitness):
    members, rank, d = a_gate.shape
    q = w_gate.shape[1]
    coeff = 1.0 / (members * lax.axis_size("z") * lax.axis_size("l") * rank) ** 0.5
    z, l, x, h, c = (lax.axis_index(a) for a in AXES)
    tok_t = tokens.T
    ag_t, au_t = (a.transpose(1, 2, 0) for a in (a_gate, a_up))
    bg, bu = (b.transpose(1, 2, 0) for b in (b_gate, b_up))
    block = (x - z - jnp.array(ORDER, jnp.int32)) % RING

    sg, su, rest = pack(tok_t, ag_t, au_t, fitness[None, :])
    bu_c = swap(bu, "c")

    def hop(axis, first, second):
        return swap(first, axis, 1), swap(second, axis, -1)

    one, three = hop("x", su, su)
    first = (2 * z + l) * 2 * d
    held = [lax.dynamic_slice_in_dim(w, first, 2 * d, 0) for w in (w_gate, w_up)]
    so = swap(rest, "h")
    one, three, bu_c, *held = join([one, three, bu_c, *held])
    at_y = (0, 2, 1, 3)
    sg_y = tie(sg, so)
    pa, pb = (
        lax.ppermute(sg_y, ("l", "h"), [(at_y[i], at_y[j]) for i, j in pairs])
        for pairs in (((1, 0), (2, 1), (0, 2)), ((3, 1), (1, 2), (2, 3)))
    )
    lo, hi, so = join([*hop("x", *halves(one, three)), so])
    su_x = (su, one, lo, hi, three)
    so = tie(so, lo)
    one, three = hop("x", so, so)
    ua = update(coeff, block, d, su_x, [bu, bu_c], so)
    gp_a, gm_a = hop("z", *ua[:2])
    one, three, pb = join([one, three, pb], ua[-1])
    lo, hi = hop("x", *halves(one, three))
    both = pick((2 * h + l).reshape(1), sg_y, pa, pb, rest, one)
    far_0 = swap(tie(bg, both), "l")
    lo, hi = join([lo, hi], both)
    so_x = (so, one, lo, hi, three)
    both = tie(both, lo)
    one, three = hop("x", both, both)
    gp_a, gm_a = join([gp_a, gm_a], both)
    ap, am = relay(gp_a, gm_a, *ua[2:4])
    fp_a, fm_a = hop("z", ap, am)
    ub = update(coeff, block, d, so_x, [bu, bu_c], ap)
    one, three = join([one, three], ap, ub[-1])
    lo, hi = hop("x", *halves(one, three))
    fp_a, fm_a = join([fp_a, fm_a], one)
    gp_b, gm_b = hop("z", *join(ub[:2], fp_a))
    lo, hi = join([lo, hi], fp_a)
    sg_x = (both, one, lo, hi, three)
    bg_c = swap(tie(bg, lo), "c")
    tok = tokens_of(jnp.stack([x, h]), sg_x, so_x, d, tok_t.shape[1], 2 * rank)
    gp_b, gm_b, far_0 = join([gp_b, gm_b, far_0], tok)
    ap, am = relay(gp_b, gm_b, *ub[2:4])
    fp_b, fm_b = hop("z", ap, am)
    fars = [v for far in (far_0,) for v in (far, swap(far, "c"))]
    tok = tie(tok, am)
    tok_c = swap(tok, "c")
    gg = update(coeff, block, d, sg_x, [bg, bg_c, *fars], ap)
    fp_b, fm_b = join([fp_b, fm_b], gg[-1])
    gp_g, gm_g = hop("z", *gg[:2])
    keep, send = up_sums(
        (l == h).astype(jnp.int32).reshape(1), (ua[4], gp_a, gm_a, fp_a, fm_a), (ub[4], gp_b, gm_b, fp_b, fm_b)
    )
    sent = swap(send, "l")
    hidden = hidden_of(c.reshape(1), tok, tok_c, w_gate.T, w_up.T, bg, bu, gg[-1])
    gp_g, gm_g = join([gp_g, gm_g], hidden)
    ap, am = relay(gp_g, gm_g, *gg[2:4])
    fp_g, fm_g = hop("z", ap, am)
    at_c = c.reshape(1)
    gate_near, gate_far = gate_early(at_c, held[0], gg[4], gp_g, gm_g, ap)
    up_near, up_far = up_sum(keep, tie(sent, gate_near))
    new_up = renew(at_c, held[1], up_near, swap(up_far, "c"))
    fp_g, fm_g = join([fp_g, fm_g], gate_near)
    gate_near, gate_far = gate_late(gate_near, gate_far, fp_g, fm_g)
    new_gate = gate_rows(at_c, held[0], gate_near, swap(gate_far, "c"))
    return hidden.T, new_gate, new_up


def solution(mesh):
    fine = Mesh(mesh.devices.reshape(4, 2, 4, 2, 2), AXES)
    pop, mp = ("z", "l"), ("x", "h", "c")
    return jax.shard_map(
        local,
        mesh=fine,
        in_specs=(
            P(pop, mp),
            P(None, mp),
            P(None, mp),
            P(pop, None, mp),
            P(pop, None, mp),
            P(pop, None, mp),
            P(pop, None, mp),
            P(pop),
        ),
        out_specs=(P(pop, mp), P(pop, mp), P(pop, mp)),
        check_vma=False,
    )
```
